32 devices in a mesh: dp: 32 (over z, y, x, core).
Axes of the slice: x: 2, y: 2, z: 4, core: 2. Of those that a mesh axis runs over, the one named last changes fastest.
Arguments:
- view_a: bfloat16 [4096, 4096], P('dp'), may hold values from -120 to 120
- view_b: bfloat16 [4096, 4096], P('dp'), may hold values from -120 to 120
Outputs:
- loss: float32 [], replicated
- grad_a: bfloat16 [4096, 4096], P('dp')
- grad_b: bfloat16 [4096, 4096], P('dp')
The draws below stay inside these ranges and needn't reach their ends.
All inputs are finite; a program needn't handle non-finite values.
Results may differ from the reference program's by a relative error of at most 0.0034.
Values may be sent and summed in bfloat16 or wider, within the bound.
No kernel may reach another device: no remote copies, remote signals or barrier semaphores. Data moves between devices by JAX's collectives and lax.ppermute only.
A program may use at most 192 MiB of HBM per device.

```python
import jax
import jax.numpy as jnp
from jax import lax

D = 4096
BATCH = 4096


def shared_part(key, rise):
    base = jax.random.normal(jax.random.fold_in(key, 101), (BATCH, D), jnp.float32)
    across = jnp.arange(D, dtype=jnp.float32) / D
    jitter = jax.random.uniform(jax.random.fold_in(key, 102), (D,), jnp.float32, -0.4, 0.4)
    gap = jnp.exp(jnp.log(0.02) * (1.0 - across) + jitter)
    along = jnp.arange(BATCH, dtype=jnp.float32) / BATCH
    wobble = jax.random.uniform(jax.random.fold_in(key, 103), (BATCH,), jnp.float32, -0.9, 0.9)
    row_scale = jnp.exp(jnp.log(rise) * along + wobble)[:, None]
    factor = jax.random.normal(jax.random.fold_in(key, 104), (BATCH, 1), jnp.float32)
    magnitude = jax.random.uniform(jax.random.fold_in(key, 105), (D,), jnp.float32, 0.3, 0.6)
    flip = jax.random.bernoulli(jax.random.fold_in(key, 106), 0.5, (D,))
    loading = jnp.where(flip, magnitude, -magnitude)
    common = base + factor * loading
    return (common, jnp.sqrt(gap), row_scale)


def draw_view_a(key, part):
    common, root, row_scale = shared_part(key, 1.7320508)
    key = jax.random.fold_in(key, 1)
    scale = jnp.exp(jax.random.uniform(jax.random.fold_in(key, 3), (D,), jnp.float32, 0.0, 1.2))
    offset = jax.random.uniform(jax.random.fold_in(key, 2), (D,), jnp.float32, -2.0, 2.0)
    noise = jax.random.normal(jax.random.fold_in(key, 4), (BATCH, D), jnp.float32)
    value = (common + root * noise) * row_scale * scale + offset
    return jnp.clip(value, -120.0, 120.0).astype(jnp.bfloat16)


def draw_view_b(key, part):
    common, root, row_scale = shared_part(key, 1.7320508)
    key = jax.random.fold_in(key, 5)
    scale = jnp.exp(jax.random.uniform(jax.random.fold_in(key, 7), (D,), jnp.float32, 0.0, 1.2))
    offset = jax.random.uniform(jax.random.fold_in(key, 6), (D,), jnp.float32, -2.0, 2.0)
    noise = jax.random.normal(jax.random.fold_in(key, 8), (BATCH, D), jnp.float32)
    value = (common + root * noise) * row_scale * scale + offset
    return jnp.clip(value, -120.0, 120.0).astype(jnp.bfloat16)


def setup_inputs(seed: int = 0) -> dict:
    splits = jax.random.split(jax.random.key(seed), 3)
    return {
        "view_a": draw_view_a(jax.random.fold_in(splits[2], 71), 0),
        "view_b": draw_view_b(jax.random.fold_in(splits[2], 71), 0),
    }


lam = 0.0051
eps = 1e-05

def normalise(view, count):
    full = view.astype(jnp.float32)
    mean = lax.optimization_barrier(jnp.sum(full, axis=0)) / count
    square = lax.optimization_barrier(jnp.sum(full * full, axis=0)) / count
    inv = 1.0 / jnp.sqrt(square - mean * mean + eps)
    flat = (full - mean) * inv
    return (flat, flat.astype(jnp.bfloat16), inv)

def backnorm(grad, flat, inv, count):
    first = lax.optimization_barrier(jnp.sum(grad, axis=0)) / count
    second = lax.optimization_barrier(jnp.sum(grad * flat, axis=0)) / count
    return (inv * (grad - first - flat * second)).astype(jnp.bfloat16)

def reference(view_a, view_b):
    count = view_a.shape[0]
    width = view_a.shape[1]
    flat_a, norm_a, inv_a = normalise(view_a, count)
    flat_b, norm_b, inv_b = normalise(view_b, count)
    corr = jnp.dot(norm_a.T, norm_b, preferred_element_type=jnp.float32) / count
    diag = jnp.diagonal(corr)
    loss = jnp.sum((1.0 - diag) ** 2) + lam * (jnp.sum(corr * corr) - jnp.sum(diag * diag))
    eye = lax.broadcasted_iota(jnp.int32, (width, width), 0) == lax.broadcasted_iota(jnp.int32, (width, width), 1)
    gcorr = jnp.where(eye, 2.0 * (corr - 1.0), 2.0 * lam * corr).astype(jnp.bfloat16)
    g_a = jnp.dot(norm_b, gcorr.T, preferred_element_type=jnp.float32)
    g_b = jnp.dot(norm_a, gcorr, preferred_element_type=jnp.float32)
    return (loss, backnorm(g_a, flat_a, inv_a, count), backnorm(g_b, flat_b, inv_b, count))
```

```python
import jax
import jax.numpy as jnp
from jax import lax
from jax.sharding import PartitionSpec as P

lam = 0.0051
eps = 1e-05

cube = 8
orders = ((4, 2, 1), (2, 1, 4), (1, 4, 2))


def offset(order, place):
    return sum(bit for step, bit in enumerate(order) if place >> step & 1)


def places(order):
    return [offset(order, place) for place in range(cube)]


def cuts(rows):
    part = -(-rows // 48) * 16
    return (0, part, 2 * part, rows)


def shards(view_a, view_b):
    f32, bf16 = jnp.float32, jnp.bfloat16
    rows, width = view_a.shape
    devices = lax.axis_size("dp")
    count = rows * devices
    cubes = devices // (2 * cube)
    index = lax.axis_index("dp")
    c, k, h = index % 2, index // 2 % cube, index // (2 * cube)
    wide, half, narrow = width // cubes, width // cubes // 2, width // cube

    def swap(x, mask):
        return lax.ppermute(x, "dp", [(i, i ^ mask) for i in range(devices)])

    def swap_k(x, bit):
        return swap(x, 2 * bit)

    def turn(x, step):
        return lax.ppermute(
            x, "dp", [(i, (i + 2 * cube * step) % devices) for i in range(devices)]
        )

    def columns(x, start, size):
        return lax.dynamic_slice_in_dim(x, start, size, axis=1)

    def pair(mine, other, axis):
        return jnp.where(
            c == 0,
            jnp.concatenate([mine, other], axis),
            jnp.concatenate([other, mine], axis),
        )

    def doubled(x, order, axis):
        for bit in order[:-1]:
            x = jnp.concatenate([x, swap_k(x, bit)], axis)
        return [x, swap_k(x, order[-1])]

    full_a, full_b = view_a.astype(f32), view_b.astype(f32)
    sums = jnp.stack(
        [
            jnp.sum(full_a, axis=0),
            jnp.sum(full_a * full_a, axis=0),
            jnp.sum(full_b, axis=0),
            jnp.sum(full_b * full_b, axis=0),
        ]
    )
    mask = 1
    while mask < devices:
        sums = sums + swap(sums, mask)
        mask *= 2
    means = sums / count
    mean_a, mean_b = means[0:1], means[2:3]
    inv_a = 1.0 / jnp.sqrt(means[1:2] - mean_a * mean_a + eps)
    inv_b = 1.0 / jnp.sqrt(means[3:4] - mean_b * mean_b + eps)

    def flat(x, mean, inv):
        return (x.astype(f32) - mean) * inv

    def norm(x, mean, inv):
        return flat(x, mean, inv).astype(bf16)

    rows_b = [view_b] + [turn(view_b, s) for s in range(1, cubes)]
    far_a = [
        turn(columns(view_a, (h + s) % cubes * wide, wide), s) for s in range(1, cubes)
    ]
    near_a = columns(view_a, h * wide, wide)
    pair_b = jnp.concatenate(rows_b, 0)
    pair_a = jnp.concatenate([near_a] + far_a, 0)

    edges = cuts(rows)
    parts = list(zip(edges, edges[1:], orders))
    own_a = [doubled(view_a[lo:hi], order, 0) for lo, hi, order in parts]
    far = jnp.concatenate(far_a, 1)
    other_a = [doubled(far[lo:hi], order, 0) for lo, hi, order in parts]
    eighths = [columns(pair_b, (k ^ r) * narrow, narrow) for r in range(cube)]
    narrow_b = [eighths[0]] + [swap_k(eighths[r], r) for r in range(1, cube)]

    def ordered_b(s):
        return jnp.concatenate(
            [
                narrow_b[r][s * rows + lo : s * rows + hi]
                for lo, hi, order in parts
                for r in places(order)
            ],
            0,
        )

    all_b = jnp.concatenate([pair_b, swap(pair_b, 1)], 0)
    all_a = jnp.concatenate(
        [columns(pair_a, c * half, half), swap(columns(pair_a, (1 - c) * half, half), 1)], 0
    )

    mean_aw, inv_aw = columns(mean_a, h * wide, wide), columns(inv_a, h * wide, wide)
    mean_bn, inv_bn = columns(mean_b, k * narrow, narrow), columns(inv_b, k * narrow, narrow)
    cube_a = norm(jnp.concatenate([x for pieces in own_a for x in pieces], 0), mean_a, inv_a)
    rest_a = jnp.concatenate([x for pieces in other_a for x in pieces], 0)
    left = jnp.concatenate(
        [columns(cube_a, h * wide, wide)]
        + [
            norm(rest_a[:, s * wide : (s + 1) * wide], mean_aw, inv_aw)
            for s in range(cubes - 1)
        ],
        0,
    )
    near_b = ordered_b(0)
    right = norm(
        jnp.concatenate([near_b] + [ordered_b(s) for s in range(1, cubes)], 0), mean_bn, inv_bn
    )
    partial = lax.dot_general(left, right, (((0,), (0,)), ((), ())), preferred_element_type=f32)
    corr = (
        lax.dynamic_slice_in_dim(partial, c * half, half, 0)
        + swap(lax.dynamic_slice_in_dim(partial, (1 - c) * half, half, 0), 1)
    ) / count
    first_i, first_j = h * wide + c * half, k * narrow
    diag = (
        lax.broadcasted_iota(jnp.int32, (half, narrow), 0) + first_i
        == lax.broadcasted_iota(jnp.int32, (half, narrow), 1) + first_j
    )
    loss = jnp.sum(jnp.where(diag, (1.0 - corr) ** 2, lam * corr * corr))
    gcorr = jnp.where(diag, 2.0 * (corr - 1.0), 2.0 * lam * corr).astype(bf16)

    loss = jnp.full((8, 128), loss, f32)
    mask = 1
    while mask < devices:
        loss = loss + swap(loss, mask)
        mask *= 2

    turned = [gcorr] + [turn(gcorr, s) for s in range(1, cubes)]
    across = jnp.zeros((cubes, half, narrow), bf16)
    for s, block in enumerate(turned):
        across = lax.dynamic_update_slice_in_dim(across, block[None], (h - s) % cubes, 0)
    sibling = swap(across, 1)
    rows_g = pair(across, sibling, 1).reshape(width, narrow)
    grad_nb = jnp.dot(cube_a, rows_g, preferred_element_type=f32)
    flat_b = flat(near_b, mean_bn, inv_bn)
    stats_b = jnp.stack([jnp.sum(grad_nb, axis=0), jnp.sum(grad_nb * flat_b, axis=0)])
    stats_b = stats_b + swap(stats_b, 1)
    mask = 2 * cube
    while mask < devices:
        stats_b = stats_b + swap(stats_b, mask)
        mask *= 2
    stats_b = stats_b / count
    out_b = (inv_bn * (grad_nb - stats_b[0:1] - flat_b * stats_b[1:2])).astype(bf16)

    norm_b = norm(all_b, mean_b, inv_b)
    edges_g = cuts(half)
    cross = []
    for lo, hi, order in zip(edges_g, edges_g[1:], orders):
        arranged = jnp.concatenate(
            [columns(norm_b, (k ^ r) * narrow, narrow) for r in places(order)], 1
        )
        pieces = doubled(gcorr[lo:hi], order, 1)
        total = 0.0
        for n, piece in enumerate(pieces):
            total = total + lax.dot_general(
                arranged[:, n * width // 2 : (n + 1) * width // 2],
                piece,
                (((1,), (1,)), ((), ())),
                preferred_element_type=f32,
            )
        cross.append(total)
    cross = jnp.concatenate(cross, 1)
    mean_ah, inv_ah = columns(mean_a, first_i, half), columns(inv_a, first_i, half)
    flat_a = flat(all_a, mean_ah, inv_ah)
    stats_a = jnp.stack([jnp.sum(cross, axis=0), jnp.sum(cross * flat_a, axis=0)])
    for bit in (1, 2, 4):
        stats_a = stats_a + swap_k(stats_a, bit)
    stats_a = stats_a / count
    out_a = (inv_ah * (cross - stats_a[0:1] - flat_a * stats_a[1:2])).astype(bf16)

    start, blocks = 0, {}
    for lo, hi, order in parts:
        for r in places(order):
            blocks.setdefault(r, []).append(out_b[start : start + hi - lo])
            start += hi - lo
    grad_b = jnp.zeros((rows, width), bf16)
    for r in range(cube):
        block = jnp.concatenate(blocks[r], 0)
        block = swap_k(block, r) if r else block
        grad_b = lax.dynamic_update_slice_in_dim(grad_b, block, (k ^ r) * narrow, 1)
    mine = cubes * rows
    both = pair(out_a[:mine], swap(out_a[mine:], 1), 1)
    grad_a = jnp.zeros((rows, width), bf16)
    for s in range(cubes):
        block = both[s * rows : (s + 1) * rows]
        block = turn(block, -s) if s else block
        grad_a = lax.dynamic_update_slice_in_dim(grad_a, block, (h + s) % cubes * wide, 1)
    return (loss[0, 0], grad_a, grad_b)


def solution(mesh):
    return jax.shard_map(
        shards,
        mesh=mesh,
        in_specs=(P("dp", None), P("dp", None)),
        out_specs=(P(), P("dp", None), P("dp", None)),
        check_vma=False,
    )
```

```python
import jax
import jax.numpy as jnp
from jax import lax
from jax.experimental import pallas as pl
from jax.experimental.pallas import tpu as pltpu
from jax.sharding import PartitionSpec as P

lam = 0.0051
eps = 1e-05

cube = 8
orders = ((4, 2, 1), (2, 1, 4), (1, 4, 2))
together = lax.optimization_barrier


def places(order):
    return [
        sum(bit for step, bit in enumerate(order) if place >> step & 1) for place in range(cube)
    ]


def stack_kernel(mean_ref, inv_ref, *refs):
    pieces, (raw_ref, norm_ref) = refs[:cube], refs[cube:]
    rows = pieces[0].shape[0]
    for r, piece in enumerate(pieces):
        raw = piece[...]
        raw_ref[0, r * rows : (r + 1) * rows, :] = raw
        norm_ref[0, r * rows : (r + 1) * rows, :] = (
            (raw.astype(jnp.float32) - mean_ref[...]) * inv_ref[...]
        ).astype(jnp.bfloat16)


def stack_blocks(pieces, rows, mean, inv):
    size, n = pieces[0].shape
    groups = size // rows
    out = jax.ShapeDtypeStruct((groups, cube * rows, n), jnp.bfloat16)
    whole = pl.BlockSpec((1, cube * rows, n), lambda g: (g, 0, 0))
    return pl.pallas_call(
        stack_kernel,
        grid=(groups,),
        out_shape=(out, out),
        in_specs=[pl.BlockSpec((1, n), lambda g: (0, 0))] * 2
        + [pl.BlockSpec((rows, n), lambda g: (g, 0))] * cube,
        out_specs=(whole, whole),
        compiler_params=pltpu.CompilerParams(vmem_limit_bytes=32 << 20),
    )(mean, inv, *pieces)


def place_kernel(k_ref, *refs):
    pieces, out_ref = refs[:cube], refs[cube]
    n = pieces[0].shape[1]
    for r, piece in enumerate(pieces):
        start = pl.multiple_of((k_ref[0] ^ r) * n, n)
        out_ref[:, pl.ds(start, n)] = piece[...]


def place_blocks(pieces, k):
    rows, n = pieces[0].shape
    vmem = pl.BlockSpec(memory_space=pltpu.VMEM)
    return pl.pallas_call(
        place_kernel,
        out_shape=jax.ShapeDtypeStruct((rows, cube * n), jnp.bfloat16),
        in_specs=[pl.BlockSpec(memory_space=pltpu.SMEM)] + [vmem] * cube,
        out_specs=vmem,
        compiler_params=pltpu.CompilerParams(vmem_limit_bytes=32 << 20),
    )(k.reshape(1), *pieces)


def shards(view_a, view_b):
    f32, bf16 = jnp.float32, jnp.bfloat16
    rows, width = view_a.shape
    devices = lax.axis_size("dp")
    count = rows * devices
    cubes = devices // (2 * cube)
    index = lax.axis_index("dp")
    c, k, h = index % 2, index // 2 % cube, index // (2 * cube)
    wide, half, narrow = width // cubes, width // cubes // 2, width // cube

    def swap(x, mask):
        return lax.ppermute(x, "dp", [(i, i ^ mask) for i in range(devices)])

    def swap_k(x, bit):
        return swap(x, 2 * bit)

    def turn(x, step):
        return lax.ppermute(
            x, "dp", [(i, (i + 2 * cube * step) % devices) for i in range(devices)]
        )

    def turns(x):
        return [turn(x, s) for s in range(1, cubes)]

    def columns(x, start, size):
        return lax.dynamic_slice_in_dim(x, start, size, axis=1)

    def pair(mine, other, axis):
        return jnp.where(
            c == 0,
            jnp.concatenate([mine, other], axis),
            jnp.concatenate([other, mine], axis),
        )

    def flat(x, mean, inv):
        return (x.astype(f32) - mean) * inv

    def norm(x, mean, inv):
        return flat(x, mean, inv).astype(bf16)

    def h_masks():
        return [2 * cube << bit for bit in range(cubes.bit_length() - 1)]

    far_raw = [turn(columns(view_a, (h + s) % cubes * wide, wide), s) for s in range(1, cubes)]

    full_a, full_b = view_a.astype(f32), view_b.astype(f32)
    sums = jnp.stack(
        [
            jnp.sum(full_a, axis=0),
            jnp.sum(full_a * full_a, axis=0),
            jnp.sum(full_b, axis=0),
            jnp.sum(full_b * full_b, axis=0),
        ]
    )
    for mask in (1, 2, 4):
        sums = sums + swap(sums, mask)
    sums, own_b = together((sums, view_b))
    own_eighths = [columns(own_b, (k ^ r) * narrow, narrow) for r in range(cube)]
    own_b = [own_eighths[0]] + [swap_k(own_eighths[r], r) for r in range(1, cube)]
    for mask in h_masks() + [8]:
        sums = sums + swap(sums, mask)
    means = sums / count
    mean_a, mean_b = means[0:1], means[2:3]
    inv_a = 1.0 / jnp.sqrt(means[1:2] - mean_a * mean_a + eps)
    inv_b = 1.0 / jnp.sqrt(means[3:4] - mean_b * mean_b + eps)
    mean_aw, inv_aw = columns(mean_a, h * wide, wide), columns(inv_a, h * wide, wide)
    mean_bn, inv_bn = columns(mean_b, k * narrow, narrow), columns(inv_b, k * narrow, narrow)

    near_raw = columns(view_a, h * wide, wide)
    norm_a = norm(view_a, mean_a, inv_a)
    near = columns(norm_a, h * wide, wide)
    rest = jnp.concatenate(
        [columns(norm_a, (h + s) % cubes * wide, wide) for s in range(1, cubes)], 1
    )
    far = jnp.concatenate([norm(x, mean_aw, inv_aw) for x in far_raw], 1)
    moving = [x.reshape(1, 1, 1, *x.shape) for x in (far, near, rest)]
    (moving, raw_b) = together((moving, view_b))
    others_b = turns(raw_b)
    far_eighths = None
    for step in range(3):
        if step == 2:
            others_b, moving = together((others_b, moving))
            pair_b = jnp.concatenate([view_b] + others_b, 0)
            outer = pair_b[rows:]
            far_eighths = [columns(outer, (k ^ r) * narrow, narrow) for r in range(cube)]
            far_b = [far_eighths[0]] + [swap_k(far_eighths[r], r) for r in range(1, cube)]
        arrived = [swap_k(x, order[step]) for x, order in zip(moving, orders)]
        moving, arrived = together((moving, arrived))
        moving = [
            jnp.concatenate([x, y], (4, 2, 1).index(order[step]))
            for x, y, order in zip(moving, arrived, orders)
        ]
    far, near, rest = [x.reshape(cube * rows, -1) for x in moving]

    near_b, right = stack_blocks(own_b, rows, mean_bn, inv_bn)
    _, rights = stack_blocks(far_b, rows, mean_bn, inv_bn)
    near_b = near_b[0]
    partial = 0.0
    for s in range(cubes):
        partial = partial + lax.dot_general(
            near if s == 0 else far[:, (s - 1) * wide : s * wide],
            right[0] if s == 0 else rights[s - 1],
            (((0,), (0,)), ((), ())),
            preferred_element_type=f32,
        )
    corr = (
        lax.dynamic_slice_in_dim(partial, c * half, half, 0)
        + swap(lax.dynamic_slice_in_dim(partial, (1 - c) * half, half, 0), 1)
    ) / count
    first_i, first_j = h * wide + c * half, k * narrow
    diag = (
        lax.broadcasted_iota(jnp.int32, (half, narrow), 0) + first_i
        == lax.broadcasted_iota(jnp.int32, (half, narrow), 1) + first_j
    )
    loss = jnp.sum(jnp.where(diag, (1.0 - corr) ** 2, lam * corr * corr))
    gcorr = jnp.where(diag, 2.0 * (corr - 1.0), 2.0 * lam * corr).astype(bf16)
    loss = jnp.full((1, narrow), loss, f32)

    all_b = jnp.concatenate([pair_b, swap(pair_b, 1)], 0)
    pair_a = jnp.concatenate([near_raw] + far_raw, 0)
    all_a = jnp.concatenate(
        [columns(pair_a, c * half, half), swap(columns(pair_a, (1 - c) * half, half), 1)], 0
    )
    norm_b = norm(all_b, mean_b, inv_b)
    arranged = [
        jnp.concatenate([columns(norm_b, (k ^ r) * narrow, narrow) for r in places(order)], 1)
        for order in orders
    ]

    part = -(-half // 48) * 16
    moving = [gcorr[:part], gcorr[part : 2 * part], gcorr[2 * part :]]
    moving, outgoing = together((moving, gcorr))
    turned = [outgoing] + turns(outgoing)
    out_b = None
    for step in range(3):
        if step == 2:
            turned, moving = together((turned, moving))
            across = jnp.zeros((cubes, half, narrow), bf16)
            for s, block in enumerate(turned):
                across = lax.dynamic_update_slice_in_dim(across, block[None], (h - s) % cubes, 0)
            rows_g = pair(across, swap(across, 1), 1).reshape(cubes, wide, narrow)

            def rows_of(s):
                return lax.dynamic_index_in_dim(rows_g, (h + s) % cubes, 0, keepdims=False)

            grad_nb = jnp.dot(near, rows_of(0), preferred_element_type=f32)
            for s in range(1, cubes):
                grad_nb = grad_nb + jnp.dot(
                    rest[:, (s - 1) * wide : s * wide], rows_of(s), preferred_element_type=f32
                )
            flat_b = flat(near_b, mean_bn, inv_bn)
            stats_b = jnp.concatenate(
                [
                    jnp.sum(grad_nb, axis=0, keepdims=True),
                    jnp.sum(grad_nb * flat_b, axis=0, keepdims=True),
                    loss,
                ]
            )
            for mask in [1] + h_masks():
                stats_b = stats_b + swap(stats_b, mask)
            first, second = stats_b[0:1] / count, stats_b[1:2] / count
            out_b = (inv_bn * (grad_nb - first - flat_b * second)).astype(bf16)
        bit = orders[0][step]
        arrived = [swap_k(x, order[step]) for x, order in zip(moving, orders)]
        if step < 2:
            loss = loss + swap_k(loss, bit)
            moving, arrived, loss = together((moving, arrived, loss))
            moving = [jnp.concatenate([x, y], 1) for x, y in zip(moving, arrived)]
            if step == 1:
                loss = loss + swap_k(loss, orders[0][2])
    moving, arrived, out_b = together((moving, arrived, out_b))
    pieces_b = [out_b[r * rows : (r + 1) * rows] for r in range(cube)]
    pieces_b = [pieces_b[0]] + [swap_k(pieces_b[r], r) for r in range(1, cube)]

    cross = jnp.concatenate(
        [
            sum(
                lax.dot_general(
                    b[:, n * width // 2 : (n + 1) * width // 2],
                    piece,
                    (((1,), (1,)), ((), ())),
                    preferred_element_type=f32,
                )
                for n, piece in enumerate((x, y))
            )
            for b, x, y in zip(arranged, moving, arrived)
        ],
        1,
    )
    mean_ah, inv_ah = columns(mean_a, first_i, half), columns(inv_a, first_i, half)
    flat_a = flat(all_a, mean_ah, inv_ah)
    stats_a = jnp.stack([jnp.sum(cross, axis=0), jnp.sum(cross * flat_a, axis=0)])
    for bit in (1, 2, 4):
        stats_a = stats_a + swap_k(stats_a, bit)
    stats_a = stats_a / count
    out_a = (inv_ah * (cross - stats_a[0:1] - flat_a * stats_a[1:2])).astype(bf16)

    grad_b = place_blocks(pieces_b, k)
    mine = cubes * rows
    both = pair(out_a[:mine], swap(out_a[mine:], 1), 1)
    grad_a = jnp.zeros((rows, width), bf16)
    for s in range(cubes):
        block = both[s * rows : (s + 1) * rows]
        block = turn(block, -s) if s else block
        grad_a = lax.dynamic_update_slice_in_dim(grad_a, block, (h + s) % cubes * wide, 1)
    return (stats_b[2, 0], grad_a, grad_b)


def solution(mesh):
    return jax.shard_map(
        shards,
        mesh=mesh,
        in_specs=(P("dp", None), P("dp", None)),
        out_specs=(P(), P("dp", None), P("dp", None)),
        check_vma=False,
    )
```

```python
import functools

import jax
import jax.numpy as jnp
from jax import lax
from jax.experimental import pallas as pl
from jax.experimental.pallas import tpu as pltpu
from jax.sharding import PartitionSpec as P

lam = 0.0051
eps = 1e-05

cube = 8
orders = ((4, 2, 1), (1, 4, 2), (2, 1, 4))
together = lax.optimization_barrier
vmem = pl.BlockSpec(memory_space=pltpu.VMEM)
smem = pl.BlockSpec(memory_space=pltpu.SMEM)
roomy = pltpu.CompilerParams(vmem_limit_bytes=32 << 20)


def places(order):
    return [
        sum(bit for step, bit in enumerate(order) if place >> step & 1) for place in range(cube)
    ]


def cuts(width):
    part = -(-width // 384) * 128
    edges = list(range(0, width, part)) + [width]
    return list(zip(edges, edges[1:]))


def prepare_kernel(half, at_ref, a_ref, b_ref, *outs):
    near_ref, rest_ref, eighths_ref, sums_ref = outs[:4]
    rows, width = a_ref.shape
    for n in range(width // half):
        column = a_ref[:, pl.ds(pl.multiple_of(at_ref[n] * half, half), half)]
        if n < 2:
            near_ref[:, n * half : (n + 1) * half] = column
        else:
            rest_ref[:, (n - 2) * half : (n - 1) * half] = column
    parts = iter(outs[4:])
    for full_ref in (near_ref, rest_ref):
        for lo, hi in cuts(full_ref.shape[1]):
            next(parts)[...] = full_ref[:, lo:hi]
    narrow = width // cube
    for i in range(cube):
        here = slice(i * narrow, (i + 1) * narrow)
        eighths_ref[i] = b_ref[:, here]
        for n, ref in enumerate((a_ref, b_ref)):
            x = ref[:, here].astype(jnp.float32)
            sums_ref[2 * n : 2 * n + 1, here] = jnp.sum(x, axis=0, keepdims=True)
            sums_ref[2 * n + 1 : 2 * n + 2, here] = jnp.sum(x * x, axis=0, keepdims=True)


def prepare(view_a, view_b, at, half):
    rows, width = view_a.shape
    widths = [2 * half, width - 2 * half]
    shapes = [(rows, n) for n in widths] + [(cube, rows, width // cube)]
    parts = [(rows, hi - lo) for n in widths for lo, hi in cuts(n)]
    outs = [jax.ShapeDtypeStruct(shape, jnp.bfloat16) for shape in shapes]
    outs += [jax.ShapeDtypeStruct((4, width), jnp.float32)]
    outs += [jax.ShapeDtypeStruct(shape, jnp.bfloat16) for shape in parts]
    near, rest, eighths, sums, *parts = pl.pallas_call(
        functools.partial(prepare_kernel, half),
        out_shape=outs,
        in_specs=[smem, vmem, vmem],
        out_specs=[vmem] * len(outs),
        compiler_params=roomy,
    )(at, view_a, view_b)
    first = len(cuts(widths[0]))
    return near, rest, eighths, sums, parts[:first], parts[first:]


def double_kernel(*refs):
    n = len(refs) // 3
    for x, y, out in zip(refs[:n], refs[n : 2 * n], refs[2 * n :]):
        rows = x.shape[0]
        out[:rows, :] = x[...]
        out[rows:, :] = y[...]


def double(xs, ys):
    return pl.pallas_call(
        double_kernel,
        out_shape=[jax.ShapeDtypeStruct((2 * x.shape[0], x.shape[1]), x.dtype) for x in xs],
        in_specs=[vmem] * (2 * len(xs)),
        out_specs=[vmem] * len(xs),
        compiler_params=roomy,
    )(*xs, *ys)


def merge_kernel(orders, mean_ref, inv_ref, *refs):
    pieces, out_ref = refs[:-1], refs[-1]
    rows = pieces[0].shape[0] * 2 // cube
    start = 0
    for n, order in enumerate(orders[: len(pieces) // 2]):
        size = pieces[2 * n].shape[1]
        mean, inv = mean_ref[:, start : start + size], inv_ref[:, start : start + size]
        for m, r in enumerate(places(order)):
            piece, first = pieces[2 * n + 2 * m // cube], m % (cube // 2) * rows
            raw = piece[first : first + rows, :].astype(jnp.float32)
            out_ref[r * rows : (r + 1) * rows, start : start + size] = (
                (raw - mean) * inv
            ).astype(jnp.bfloat16)
        start += size


def merge(moving, arrived, orders, mean, inv):
    pieces = [x for pair in zip(moving, arrived) for x in pair]
    return pl.pallas_call(
        functools.partial(merge_kernel, orders),
        out_shape=jax.ShapeDtypeStruct((2 * pieces[0].shape[0], mean.shape[1]), jnp.bfloat16),
        in_specs=[vmem] * (2 + len(pieces)),
        out_specs=vmem,
        compiler_params=roomy,
    )(mean, inv, *pieces)


def arrange_kernel(k_ref, blocks_ref, mean_ref, inv_ref, raw_ref, norm_ref):
    rows = blocks_ref.shape[1]
    for r in range(cube):
        raw = blocks_ref[k_ref[0] ^ r]
        raw_ref[r * rows : (r + 1) * rows, :] = raw
        norm_ref[r * rows : (r + 1) * rows, :] = (
            (raw.astype(jnp.float32) - mean_ref[...]) * inv_ref[...]
        ).astype(jnp.bfloat16)


def arrange(blocks, mean, inv, k):
    _, rows, n = blocks.shape
    out = jax.ShapeDtypeStruct((cube * rows, n), jnp.bfloat16)
    return pl.pallas_call(
        arrange_kernel,
        out_shape=(out, out),
        in_specs=[smem] + [vmem] * 3,
        out_specs=(vmem, vmem),
        compiler_params=roomy,
    )(k.reshape(1), blocks, mean, inv)


def finish_kernel(k_ref, grad_ref, raw_ref, mean_ref, inv_ref, first_ref, second_ref, out_ref):
    rows = out_ref.shape[1]
    mean, inv = mean_ref[...], inv_ref[...]
    for r in range(cube):
        here = slice(r * rows, (r + 1) * rows)
        flat = (raw_ref[here, :].astype(jnp.float32) - mean) * inv
        out = inv * (grad_ref[here, :] - first_ref[...] - flat * second_ref[...])
        out_ref[k_ref[0] ^ r] = out.astype(jnp.bfloat16)


def finish(grad, raw, mean, inv, first, second, k):
    size, n = grad.shape
    return pl.pallas_call(
        finish_kernel,
        out_shape=jax.ShapeDtypeStruct((cube, size // cube, n), jnp.bfloat16),
        in_specs=[smem] + [vmem] * 6,
        out_specs=vmem,
        compiler_params=roomy,
    )(k.reshape(1), grad, raw, mean, inv, first, second)


def place_kernel(at_ref, *refs):
    blocks, out_ref = refs[:-1], refs[-1]
    half = blocks[0].shape[1] // 2
    for n, block in enumerate(blocks):
        for side in range(2):
            start = pl.multiple_of(at_ref[2 * n + side] * half, half)
            out_ref[:, pl.ds(start, half)] = block[:, side * half : (side + 1) * half]


def place(blocks, at):
    rows, n = blocks[0].shape
    return pl.pallas_call(
        place_kernel,
        out_shape=jax.ShapeDtypeStruct((rows, n * len(blocks)), jnp.bfloat16),
        in_specs=[smem] + [vmem] * len(blocks),
        out_specs=vmem,
        compiler_params=roomy,
    )(at, *blocks)


def dot(x, y, contract):
    return lax.dot_general(x, y, (contract, ((), ())), preferred_element_type=jnp.float32)


def cross_kernel(orders, k_ref, raw_ref, mean_ref, inv_ref, rows_ref, *refs):
    pieces, (out_ref, sums_ref) = refs[:-2], refs[-2:]
    narrow = rows_ref.shape[1] // cube
    start = 0
    for n, order in enumerate(orders[: len(pieces) // 2]):
        size = pieces[2 * n].shape[1]
        total = 0.0
        for m, r in enumerate(places(order)):
            piece = pieces[2 * n + 2 * m // cube]
            first = m % (cube // 2) * narrow
            at = pl.multiple_of((k_ref[0] ^ r) * narrow, narrow)
            total = total + jnp.dot(
                rows_ref[:, pl.ds(at, narrow)],
                piece[first : first + narrow, :],
                preferred_element_type=jnp.float32,
            )
        out_ref[:, start : start + size] = total
        start += size
    out = out_ref[...]
    flat = (raw_ref[...].astype(jnp.float32) - mean_ref[...]) * inv_ref[...]
    sums = jnp.concatenate(
        [jnp.sum(out, axis=0, keepdims=True), jnp.sum(out * flat, axis=0, keepdims=True)]
    )

    @pl.when(pl.program_id(0) == 0)
    def _():
        sums_ref[...] = sums

    @pl.when(pl.program_id(0) > 0)
    def _():
        sums_ref[...] += sums


def cross_products(rows, pieces, orders, raw, mean, inv, k):
    size, n = raw.shape
    block = min(size, 512)

    def whole(x):
        return pl.BlockSpec(x.shape, lambda i: (0, 0))

    def part(x):
        return pl.BlockSpec((block, x.shape[1]), lambda i: (i, 0))

    return pl.pallas_call(
        functools.partial(cross_kernel, orders),
        grid=(size // block,),
        out_shape=(
            jax.ShapeDtypeStruct((size, n), jnp.float32),
            jax.ShapeDtypeStruct((2, n), jnp.float32),
        ),
        in_specs=[smem, part(raw), whole(mean), whole(inv), part(rows)]
        + [whole(x) for x in pieces],
        out_specs=(part(raw), pl.BlockSpec((2, n), lambda i: (0, 0))),
        compiler_params=pltpu.CompilerParams(vmem_limit_bytes=48 << 20),
    )(k.reshape(1), raw, mean, inv, rows, *pieces)


def shards(view_a, view_b):
    f32, bf16 = jnp.float32, jnp.bfloat16
    rows, width = view_a.shape
    devices = lax.axis_size("dp")
    count = rows * devices
    cubes = devices // (2 * cube)
    index = lax.axis_index("dp")
    c, k, h = index % 2, index // 2 % cube, index // (2 * cube)
    wide, half, narrow = width // cubes, width // cubes // 2, width // cube
    groups = [
        [(g * cube + i) * 2 + core for i in range(cube)] for g in range(cubes) for core in range(2)
    ]

    def swap(x, mask):
        return lax.ppermute(x, "dp", [(i, i ^ mask) for i in range(devices)])

    def swap_k(x, bit):
        return swap(x, 2 * bit)

    def turn(x, step):
        return lax.ppermute(
            x, "dp", [(i, (i + 2 * cube * step) % devices) for i in range(devices)]
        )

    def turns(x):
        return [turn(x, s) for s in range(1, cubes)]

    def exchange(x):
        return lax.all_to_all(
            x, "dp", split_axis=0, concat_axis=0, axis_index_groups=groups, tiled=True
        )

    def columns(x, start, size):
        return lax.dynamic_slice_in_dim(x, start, size, axis=1)

    at = [(h + s) % cubes * 2 + core for s in range(cubes) for core in (c, 1 - c)]

    h_masks = [2 * cube << bit for bit in range(cubes.bit_length() - 1)]

    def by_place(x, sides):
        return jnp.concatenate([columns(x, place * half, half) for place in sides], 1)

    def send(moving, step):
        return [swap_k(x, order[step]) for x, order in zip(moving, orders)]

    whole_near, whole_rest, eighths, sums, near, rest = prepare(view_a, view_b, jnp.stack(at), half)
    parts_a = [whole_near] + [whole_rest[:, s * wide : (s + 1) * wide] for s in range(cubes - 1)]
    cuts_b = (0, 3 * rows // 8, 3 * rows // 4, rows)
    pieces_b = [view_b[lo:hi] for lo, hi in zip(cuts_b, cuts_b[1:])]
    others_b = []

    arrived = send(rest, 0)
    for mask in (1, 2, 4):
        sums = sums + swap(sums, mask)
    rest, arrived, sums, pieces_b, near, eighths = together(
        (rest, arrived, sums, pieces_b, near, eighths)
    )
    rest = double(rest, arrived)
    arrived = send(rest, 1)
    own_b = exchange(eighths)
    others_b.append(turns(pieces_b[0]))
    for mask in h_masks + [8]:
        sums = sums + swap(sums, mask)
    rest, arrived, others_b, sums, pieces_b, own_b = together(
        (rest, arrived, others_b, sums, pieces_b, own_b)
    )
    rest = double(rest, arrived)
    arrived = send(rest, 2)
    others_b.append(turns(pieces_b[1]))
    means = sums / count
    mean_a, mean_b = means[0:1], means[2:3]
    inv_a = 1.0 / jnp.sqrt(means[1:2] - mean_a * mean_a + eps)
    inv_b = 1.0 / jnp.sqrt(means[3:4] - mean_b * mean_b + eps)
    mean_bn = columns(mean_b, k * narrow, narrow)
    inv_bn = columns(inv_b, k * narrow, narrow)
    mean_ap, inv_ap = by_place(mean_a, at), by_place(inv_a, at)
    near_b, right = arrange(own_b, mean_bn, inv_bn, k)
    rest, arrived, others_b, pieces_b, near_b, right, mean_ap, inv_ap = together(
        (rest, arrived, others_b, pieces_b, near_b, right, mean_ap, inv_ap)
    )

    def product(left, s):
        first = dot(right, left[:, s * wide + half : (s + 1) * wide], ((0,), (0,)))
        return swap(first, 1) + dot(right, left[:, s * wide : s * wide + half], ((0,), (0,)))

    def diagonal(s):
        return (
            lax.broadcasted_iota(jnp.int32, (narrow, half), 1) + at[2 * s] * half
            == lax.broadcasted_iota(jnp.int32, (narrow, half), 0) + k * narrow
        )

    rest = merge(rest, arrived, orders, mean_ap[:, wide:], inv_ap[:, wide:])
    others_b.append(turns(pieces_b[2]))
    arrived = send(near, 0)
    partials = [product(rest, s) for s in range(cubes - 1)]
    exact = [
        jnp.sum(jnp.where(diagonal(s + 1), x, 0.0), axis=1).reshape(1, narrow)
        for s, x in enumerate(partials)
    ]
    partials = [x.astype(bf16) for x in partials]
    partials, exact, near, arrived, others_b = together(
        (partials, exact, near, arrived, others_b)
    )
    near = double(near, arrived)

    cuts_p = (0, narrow // 4, 5 * narrow // 8, narrow)
    received = []
    for step in (1, 2):
        arrived = send(near, step)
        received.append(
            [turn(x[cuts_p[step - 1] : cuts_p[step]], s + 1) for s, x in enumerate(partials)]
        )
        if step == 1:
            near, arrived, received, partials, exact = together(
                (near, arrived, received, partials, exact)
            )
            near = double(near, arrived)
        else:
            exact = [turn(x, s + 1) for s, x in enumerate(exact)]
            others_b = [jnp.concatenate(pieces, 0) for pieces in zip(*others_b)]
            pair_b = jnp.concatenate([view_b] + others_b, 0)
            pair_b = ((pair_b.astype(f32) - mean_b) * inv_b).astype(bf16)
            norm_b = jnp.concatenate([pair_b, swap(pair_b, 1)], 0)
            near, arrived, received, partials, exact, norm_b = together(
                (near, arrived, received, partials, exact, norm_b)
            )
    received.append([turn(x[cuts_p[2] :], s + 1) for s, x in enumerate(partials)])
    near = merge(near, arrived, orders, mean_ap[:, :wide], inv_ap[:, :wide])
    corr = product(near, 0)
    corr, received = together((corr, received))
    diag = diagonal(0)
    for blocks, line in zip(zip(*received), exact):
        block = jnp.concatenate(blocks, 0).astype(f32)
        corr = corr + jnp.where(diag, line.reshape(narrow, 1), block)
    corr = corr / count
    loss = jnp.sum(jnp.where(diag, (1.0 - corr) ** 2, lam * corr * corr))
    gcorr = jnp.where(diag, 2.0 * (corr - 1.0), 2.0 * lam * corr).astype(bf16)

    moving = [gcorr[:, lo:hi] for lo, hi in cuts(half)]
    cuts_g = (0, narrow // 4, 5 * narrow // 8, narrow)
    loss = jnp.full((8, 128), loss, f32)
    turned, sibling, far_a = [], [], []
    for step in range(3):
        arrived = send(moving, step)
        turned.append(turns(gcorr[cuts_g[step] : cuts_g[step + 1]]))
        if step > 0:
            sibling.append([swap(x, 1) for x in turned[step - 1]])
            far_a.append(
                [
                    turn(x[:, (2 - step) * half : (3 - step) * half], s + 1)
                    for s, x in enumerate(parts_a[1:])
                ]
            )
        if step == 0:
            own = jnp.concatenate([gcorr, swap(gcorr, 1)], 1)
            loss = loss + swap(loss, 1)
            moving, arrived, turned, gcorr, own, loss, parts_a = together(
                (moving, arrived, turned, gcorr, own, loss, parts_a)
            )
        elif step == 1:
            grad_nb = dot(near, own, ((1,), (1,)))
            moving, arrived, turned, gcorr, sibling, far_a, parts_a, grad_nb = together(
                (moving, arrived, turned, gcorr, sibling, far_a, parts_a, grad_nb)
            )
        else:
            other_a = swap(jnp.concatenate([parts_a[0][:, half:]] + far_a[0], 0), 1)
            moving, arrived, turned, sibling, far_a, other_a, loss = together(
                (moving, arrived, turned, sibling, far_a, other_a, loss)
            )
        if step < 2:
            moving = double(moving, arrived)

    mean_ah, inv_ah = mean_ap[:, :half], inv_ap[:, :half]
    sibling.append([swap(x, 1) for x in turned[2]])
    all_a = jnp.concatenate([parts_a[0][:, :half]] + far_a[1] + [other_a], 0)
    pieces = [x for pair in zip(moving, arrived) for x in pair]
    cross, stats_a = cross_products(norm_b, pieces, orders, all_a, mean_ah, inv_ah, k)
    for mask in h_masks:
        loss = loss + swap(loss, mask)
    cross, stats_a, sibling, loss = together((cross, stats_a, sibling, loss))
    stats_a = jnp.concatenate([stats_a, jnp.full((1, half), loss[0, 0], f32)])
    for bit in (1, 2, 4):
        stats_a = stats_a + swap_k(stats_a, bit)

    for s in range(1, cubes):
        for side, blocks in enumerate((turned, sibling)):
            block = jnp.concatenate([x[cubes - s - 1] for x in blocks], 0)
            start = (s - 1) * wide + side * half
            grad_nb = grad_nb + dot(rest[:, start : start + half], block, ((1,), (1,)))
    flat_b = (near_b.astype(f32) - mean_bn) * inv_bn
    stats_b = jnp.stack([jnp.sum(grad_nb, axis=0), jnp.sum(grad_nb * flat_b, axis=0)])
    for mask in [1] + h_masks:
        stats_b = stats_b + swap(stats_b, mask)
    stats_a, stats_b, grad_nb = together((stats_a, stats_b, grad_nb))
    loss = stats_a[2, 0]
    stats_a, stats_b = stats_a / count, stats_b / count

    flat_a = (all_a.astype(f32) - mean_ah) * inv_ah
    out_a = (inv_ah * (cross - stats_a[0:1] - flat_a * stats_a[1:2])).astype(bf16)
    mine = cubes * rows
    both = jnp.concatenate([out_a[:mine], swap(out_a[mine:], 1)], 1)
    blocks = [both[s * rows : (s + 1) * rows] for s in range(cubes)]
    blocks = [blocks[0]] + [turn(blocks[s], -s) for s in range(1, cubes)]
    grad_a = place(blocks, jnp.stack(at))
    out_b = exchange(finish(grad_nb, near_b, mean_bn, inv_bn, stats_b[0:1], stats_b[1:2], k))
    grad_b = jnp.concatenate([out_b[r] for r in range(cube)], 1)
    return (loss, grad_a, grad_b)


def solution(mesh):
    return jax.shard_map(
        shards,
        mesh=mesh,
        in_specs=(P("dp", None), P("dp", None)),
        out_specs=(P(), P("dp", None), P("dp", None)),
        check_vma=False,
    )
```

```python
import functools
import math

import jax
import jax.numpy as jnp
from jax import lax
from jax.experimental import pallas as pl
from jax.experimental.pallas import tpu as pltpu
from jax.sharding import PartitionSpec as P

lam = 0.0051
eps = 1e-05

cube = 8
orders = ((4, 2, 1), (1, 4, 2), (2, 1, 4))
together = lax.optimization_barrier
vmem = pl.BlockSpec(memory_space=pltpu.VMEM)
smem = pl.BlockSpec(memory_space=pltpu.SMEM)


def room(*arrays):
    sizes = [math.prod(x.shape) * x.dtype.itemsize for x in arrays]
    return pltpu.CompilerParams(vmem_limit_bytes=sum(sizes) + max(sizes) + (4 << 20))


def places(order):
    return [
        sum(bit for step, bit in enumerate(order) if place >> step & 1) for place in range(cube)
    ]


def cuts(width):
    part = -(-width // 384) * 128
    edges = list(range(0, width, part)) + [width]
    return list(zip(edges, edges[1:]))


def prepare_kernel(half, at_ref, a_ref, b_ref, *outs):
    near_ref, rest_ref, eighths_ref, sums_ref = outs[:4]
    rows, width = a_ref.shape
    for n in range(width // half):
        column = a_ref[:, pl.ds(pl.multiple_of(at_ref[n] * half, half), half)]
        if n < 2:
            near_ref[:, n * half : (n + 1) * half] = column
        else:
            rest_ref[:, (n - 2) * half : (n - 1) * half] = column
    parts = iter(outs[4:])
    for full_ref in (near_ref, rest_ref):
        for lo, hi in cuts(full_ref.shape[1]):
            next(parts)[...] = full_ref[:, lo:hi]
    narrow = width // cube
    for i in range(cube):
        here = slice(i * narrow, (i + 1) * narrow)
        eighths_ref[i] = b_ref[:, here]
        for n, ref in enumerate((a_ref, b_ref)):
            x = ref[:, here].astype(jnp.float32)
            sums_ref[2 * n : 2 * n + 1, here] = jnp.sum(x, axis=0, keepdims=True)
            sums_ref[2 * n + 1 : 2 * n + 2, here] = jnp.sum(x * x, axis=0, keepdims=True)


def prepare(view_a, view_b, at, half):
    rows, width = view_a.shape
    widths = [2 * half, width - 2 * half]
    shapes = [(rows, n) for n in widths] + [(cube, rows, width // cube)]
    parts = [(rows, hi - lo) for n in widths for lo, hi in cuts(n)]
    outs = [jax.ShapeDtypeStruct(shape, jnp.bfloat16) for shape in shapes]
    outs += [jax.ShapeDtypeStruct((4, width), jnp.float32)]
    outs += [jax.ShapeDtypeStruct(shape, jnp.bfloat16) for shape in parts]
    near, rest, eighths, sums, *parts = pl.pallas_call(
        functools.partial(prepare_kernel, half),
        out_shape=outs,
        in_specs=[smem, vmem, vmem],
        out_specs=[vmem] * len(outs),
        compiler_params=room(view_a, view_b, *outs),
    )(at, view_a, view_b)
    first = len(cuts(widths[0]))
    return near, rest, eighths, sums, parts[:first], parts[first:]


def double_kernel(*refs):
    n = len(refs) // 3
    for x, y, out in zip(refs[:n], refs[n : 2 * n], refs[2 * n :]):
        rows = x.shape[0]
        out[:rows, :] = x[...]
        out[rows:, :] = y[...]


def double(xs, ys):
    return pl.pallas_call(
        double_kernel,
        out_shape=[jax.ShapeDtypeStruct((2 * x.shape[0], x.shape[1]), x.dtype) for x in xs],
        in_specs=[vmem] * (2 * len(xs)),
        out_specs=[vmem] * len(xs),
        compiler_params=room(*xs, *ys, *xs, *ys),
    )(*xs, *ys)


def merge_kernel(orders, mean_ref, inv_ref, *refs):
    pieces, out_ref = refs[:-1], refs[-1]
    rows = pieces[0].shape[0] * 2 // cube
    start = 0
    for n, order in enumerate(orders[: len(pieces) // 2]):
        size = pieces[2 * n].shape[1]
        mean, inv = mean_ref[:, start : start + size], inv_ref[:, start : start + size]
        for m, r in enumerate(places(order)):
            piece, first = pieces[2 * n + 2 * m // cube], m % (cube // 2) * rows
            raw = piece[first : first + rows, :].astype(jnp.float32)
            out_ref[r * rows : (r + 1) * rows, start : start + size] = (
                (raw - mean) * inv
            ).astype(jnp.bfloat16)
        start += size


def merge(moving, arrived, orders, mean, inv):
    pieces = [x for pair in zip(moving, arrived) for x in pair]
    return pl.pallas_call(
        functools.partial(merge_kernel, orders),
        out_shape=jax.ShapeDtypeStruct((2 * pieces[0].shape[0], mean.shape[1]), jnp.bfloat16),
        in_specs=[vmem] * (2 + len(pieces)),
        out_specs=vmem,
        compiler_params=room(*pieces, *pieces),
    )(mean, inv, *pieces)


def arrange_kernel(k_ref, blocks_ref, mean_ref, inv_ref, raw_ref, norm_ref):
    rows = blocks_ref.shape[1]
    for r in range(cube):
        raw = blocks_ref[k_ref[0] ^ r]
        raw_ref[r * rows : (r + 1) * rows, :] = raw
        norm_ref[r * rows : (r + 1) * rows, :] = (
            (raw.astype(jnp.float32) - mean_ref[...]) * inv_ref[...]
        ).astype(jnp.bfloat16)


def arrange(blocks, mean, inv, k):
    _, rows, n = blocks.shape
    out = jax.ShapeDtypeStruct((cube * rows, n), jnp.bfloat16)
    return pl.pallas_call(
        arrange_kernel,
        out_shape=(out, out),
        in_specs=[smem] + [vmem] * 3,
        out_specs=(vmem, vmem),
        compiler_params=room(blocks, out, out),
    )(k.reshape(1), blocks, mean, inv)


def finish_kernel(k_ref, grad_ref, raw_ref, mean_ref, inv_ref, first_ref, second_ref, out_ref):
    rows = out_ref.shape[1]
    mean, inv = mean_ref[...], inv_ref[...]
    for r in range(cube):
        here = slice(r * rows, (r + 1) * rows)
        flat = (raw_ref[here, :].astype(jnp.float32) - mean) * inv
        out = inv * (grad_ref[here, :] - first_ref[...] - flat * second_ref[...])
        out_ref[k_ref[0] ^ r] = out.astype(jnp.bfloat16)


def finish(grad, raw, mean, inv, first, second, k):
    size, n = grad.shape
    return pl.pallas_call(
        finish_kernel,
        out_shape=jax.ShapeDtypeStruct((cube, size // cube, n), jnp.bfloat16),
        in_specs=[smem] + [vmem] * 6,
        out_specs=vmem,
        compiler_params=room(grad, raw, raw),
    )(k.reshape(1), grad, raw, mean, inv, first, second)


def place_kernel(at_ref, *refs):
    blocks, out_ref = refs[:-1], refs[-1]
    half = blocks[0].shape[1] // 2
    for n, block in enumerate(blocks):
        for side in range(2):
            start = pl.multiple_of(at_ref[2 * n + side] * half, half)
            out_ref[:, pl.ds(start, half)] = block[:, side * half : (side + 1) * half]


def place(blocks, at):
    rows, n = blocks[0].shape
    return pl.pallas_call(
        place_kernel,
        out_shape=jax.ShapeDtypeStruct((rows, n * len(blocks)), jnp.bfloat16),
        in_specs=[smem] + [vmem] * len(blocks),
        out_specs=vmem,
        compiler_params=room(*blocks, *blocks),
    )(at, *blocks)


def dot(x, y, contract):
    return lax.dot_general(x, y, (contract, ((), ())), preferred_element_type=jnp.float32)


def cross_kernel(side, orders, k_ref, rows_ref, *refs):
    if side == 0:
        pieces, out_ref = refs[:-1], refs[-1]
    else:
        total_ref, raw_ref, mean_ref, inv_ref, *pieces, out_ref, sums_ref = refs
    narrow = rows_ref.shape[1] // cube
    start = 0
    for order, piece in zip(orders, pieces):
        here = slice(start, start + piece.shape[1])
        start += piece.shape[1]
        total = 0.0 if side == 0 else total_ref[:, here]
        for m in range(cube // 2):
            r = places(order)[side * cube // 2 + m]
            at = pl.multiple_of((k_ref[0] ^ r) * narrow, narrow)
            total = total + jnp.dot(
                rows_ref[:, pl.ds(at, narrow)],
                piece[m * narrow : (m + 1) * narrow, :],
                preferred_element_type=jnp.float32,
            )
        out_ref[:, here] = total
        if side == 1:
            flat = (raw_ref[:, here].astype(jnp.float32) - mean_ref[:, here]) * inv_ref[:, here]
            sums_ref[0, 0:1, here] = jnp.sum(total, axis=0, keepdims=True)
            sums_ref[0, 1:2, here] = jnp.sum(total * flat, axis=0, keepdims=True)


def cross_products(side, rows, pieces, orders, k, *more):
    size, n = rows.shape[0], sum(x.shape[1] for x in pieces)
    block = min(size, 512)

    def whole(x):
        return pl.BlockSpec(x.shape, lambda i: (0, 0))

    def part(x):
        return pl.BlockSpec((block, x.shape[1]), lambda i: (i, 0))

    out = jax.ShapeDtypeStruct((size, n), jnp.float32)
    sums = jax.ShapeDtypeStruct((size // block, 2, n), jnp.float32)
    specs = [part(x) if x.shape[0] == size else whole(x) for x in more]
    return pl.pallas_call(
        functools.partial(cross_kernel, side, orders),
        grid=(size // block,),
        out_shape=(out, sums) if side else out,
        in_specs=[smem, part(rows)] + specs + [whole(x) for x in pieces],
        out_specs=(part(out), pl.BlockSpec((1, 2, n), lambda i: (i, 0, 0))) if side else part(out),
        compiler_params=pltpu.CompilerParams(vmem_limit_bytes=48 << 20),
    )(k.reshape(1), rows, *more, *pieces)


def shards(view_a, view_b):
    f32, bf16 = jnp.float32, jnp.bfloat16
    rows, width = view_a.shape
    devices = lax.axis_size("dp")
    count = rows * devices
    cubes = devices // (2 * cube)
    index = lax.axis_index("dp")
    c, k, h = index % 2, index // 2 % cube, index // (2 * cube)
    wide, half, narrow = width // cubes, width // cubes // 2, width // cube
    groups = [
        [(g * cube + i) * 2 + core for i in range(cube)] for g in range(cubes) for core in range(2)
    ]

    def swap(x, mask):
        return lax.ppermute(x, "dp", [(i, i ^ mask) for i in range(devices)])

    def swap_k(x, bit):
        return swap(x, 2 * bit)

    def turn(x, step):
        return lax.ppermute(
            x, "dp", [(i, (i + 2 * cube * step) % devices) for i in range(devices)]
        )

    def turns(x):
        return [turn(x, s) for s in range(1, cubes)]

    def exchange(x):
        return lax.all_to_all(
            x, "dp", split_axis=0, concat_axis=0, axis_index_groups=groups, tiled=True
        )

    def columns(x, start, size):
        return lax.dynamic_slice_in_dim(x, start, size, axis=1)

    at = [(h + s) % cubes * 2 + core for s in range(cubes) for core in (c, 1 - c)]

    h_masks = [2 * cube << bit for bit in range(cubes.bit_length() - 1)]

    def by_place(x, sides):
        return jnp.concatenate([columns(x, place * half, half) for place in sides], 1)

    def send(moving, step):
        return [swap_k(x, order[step]) for x, order in zip(moving, orders)]

    whole_near, whole_rest, eighths, sums, near, rest = prepare(view_a, view_b, jnp.stack(at), half)
    parts_a = [whole_near] + [whole_rest[:, s * wide : (s + 1) * wide] for s in range(cubes - 1)]
    cuts_b = (0, rows // 2, rows)
    pieces_b = [view_b[lo:hi] for lo, hi in zip(cuts_b, cuts_b[1:])]
    others_b = []

    arrived = send(rest, 0)

    own_b = exchange(eighths)
    far_1 = [turn(x[:, half:], s + 1) for s, x in enumerate(parts_a[1:])]
    for mask in [1] + h_masks:
        sums = sums + swap(sums, mask)
    rest, arrived, sums, pieces_b, near, parts_a, far_1 = together(
        (rest, arrived, sums, pieces_b, near, parts_a, far_1)
    )
    rest = double(rest, arrived)
    arrived = send(rest, 1)
    others_b.append(turns(pieces_b[0]))
    for mask in (2, 4):
        sums = sums + swap(sums, mask)
    rest, arrived, others_b, sums, pieces_b, own_b, parts_a, far_1 = together(
        (rest, arrived, others_b, sums, pieces_b, own_b, parts_a, far_1)
    )
    rest = double(rest, arrived)
    arrived = send(rest, 2)
    others_b.append(turns(pieces_b[1]))
    sums = sums + swap(sums, 8)
    means = sums / count
    mean_a, mean_b = means[0:1], means[2:3]
    inv_a = 1.0 / jnp.sqrt(means[1:2] - mean_a * mean_a + eps)
    inv_b = 1.0 / jnp.sqrt(means[3:4] - mean_b * mean_b + eps)
    mean_bn = columns(mean_b, k * narrow, narrow)
    inv_bn = columns(inv_b, k * narrow, narrow)
    mean_ap, inv_ap = by_place(mean_a, at), by_place(inv_a, at)
    near_b, right = arrange(own_b, mean_bn, inv_bn, k)
    rest, arrived, others_b, near_b, right, mean_ap, inv_ap, parts_a, far_1 = together(
        (rest, arrived, others_b, near_b, right, mean_ap, inv_ap, parts_a, far_1)
    )

    def product(left, s):
        first = dot(right, left[:, s * wide + half : (s + 1) * wide], ((0,), (0,)))
        return swap(first, 1) + dot(right, left[:, s * wide : s * wide + half], ((0,), (0,)))

    def diagonal(s):
        return (
            lax.broadcasted_iota(jnp.int32, (narrow, half), 1) + at[2 * s] * half
            == lax.broadcasted_iota(jnp.int32, (narrow, half), 0) + k * narrow
        )

    rest = merge(rest, arrived, orders, mean_ap[:, wide:], inv_ap[:, wide:])
    arrived = send(near, 0)
    partials = [product(rest, s) for s in range(cubes - 1)]
    exact = [
        jnp.sum(jnp.where(diagonal(s + 1), x, 0.0), axis=1).reshape(1, narrow)
        for s, x in enumerate(partials)
    ]
    partials = [x.astype(bf16) for x in partials]
    partials, exact, near, arrived, others_b = together(
        (partials, exact, near, arrived, others_b)
    )
    near = double(near, arrived)

    cuts_p = (0, 3 * narrow // 8, 7 * narrow // 8, narrow)
    received = []
    for step in (1, 2):
        arrived = send(near, step)
        received.append(
            [turn(x[cuts_p[step - 1] : cuts_p[step]], s + 1) for s, x in enumerate(partials)]
        )
        if step == 1:
            other_a = swap(jnp.concatenate([parts_a[0][:, half:]] + far_1, 0), 1)
            near, arrived, received, partials, exact, others_b, other_a = together(
                (near, arrived, received, partials, exact, others_b, other_a)
            )
            near = double(near, arrived)
        else:
            others_b = [jnp.concatenate(pieces, 0) for pieces in zip(*others_b)]
            pair_b = jnp.concatenate([view_b] + others_b, 0)
            pair_b = ((pair_b.astype(f32) - mean_b) * inv_b).astype(bf16)
            near, arrived, received, partials, exact, pair_b = together(
                (near, arrived, received, partials, exact, pair_b)
            )
    received.append([turn(x[cuts_p[2] :], s + 1) for s, x in enumerate(partials)])
    exact = [turn(x, s + 1) for s, x in enumerate(exact)]
    near = merge(near, arrived, orders, mean_ap[:, :wide], inv_ap[:, :wide])
    corr = product(near, 0)
    corr, received, exact = together((corr, received, exact))
    diag = diagonal(0)
    for blocks, line in zip(zip(*received), exact):
        block = jnp.concatenate(blocks, 0).astype(f32)
        corr = corr + jnp.where(diag, line.reshape(narrow, 1), block)
    corr = corr / count
    loss = jnp.sum(jnp.where(diag, (1.0 - corr) ** 2, lam * corr * corr))
    gcorr = jnp.where(diag, 2.0 * (corr - 1.0), 2.0 * lam * corr).astype(bf16)

    moving = [gcorr[:, lo:hi] for lo, hi in cuts(half)]
    loss = jnp.full((8, 128), loss, f32)
    cuts_g = (0, narrow // 4, 3 * narrow // 4, narrow)
    mean_ah, inv_ah = mean_ap[:, :half], inv_ap[:, :half]
    turned, sibling = [], []
    for step in range(3):
        arrived = send(moving, step)
        piece = gcorr[cuts_g[step] : cuts_g[step + 1]]
        if step < 2:
            turned.append(turns(piece))
        else:
            both = [
                turn(jnp.concatenate([piece, x[:, :half]], 0), s + 1)
                for s, x in enumerate(parts_a[1:])
            ]
            turned.append([x[: narrow // 4] for x in both])
            far_0 = [x[narrow // 4 :] for x in both]
        if step > 0:
            sibling.append([swap(x, 1) for x in turned[step - 1]])
        if step == 0:
            for mask in [1] + h_masks:
                loss = loss + swap(loss, mask)
            moving, arrived, turned, gcorr, parts_a, pair_b, loss = together(
                (moving, arrived, turned, gcorr, parts_a, pair_b, loss)
            )
        elif step == 1:
            norm_b = jnp.concatenate([pair_b, swap(pair_b, 1)], 0)
            own = jnp.concatenate([gcorr, swap(gcorr, 1)], 1)
            moving, arrived, turned, gcorr, sibling, parts_a, norm_b, own = together(
                (moving, arrived, turned, gcorr, sibling, parts_a, norm_b, own)
            )
        else:
            cross = cross_products(0, norm_b, moving, orders, k)
            grad_nb = dot(near, own, ((1,), (1,)))
            arrived, turned, sibling, far_0, cross, mean_ah, inv_ah, grad_nb = together(
                (arrived, turned, sibling, far_0, cross, mean_ah, inv_ah, grad_nb)
            )
        if step < 2:
            moving = double(moving, arrived)

    sibling.append([swap(x, 1) for x in turned[2]])
    all_a = jnp.concatenate([parts_a[0][:, :half]] + far_0 + [other_a], 0)
    cross, stats_a = cross_products(
        1, norm_b, arrived, orders, k, cross, all_a, mean_ah, inv_ah
    )
    cross, stats_a, sibling, rest = together((cross, stats_a, sibling, rest))
    stats_a = jnp.concatenate(
        [jnp.sum(stats_a, axis=0), jnp.broadcast_to(loss[0:1, 0:1], (1, half))]
    )
    stats_a = stats_a + swap_k(stats_a, 1)

    for s in range(1, cubes):
        for side, blocks in enumerate((turned, sibling)):
            block = jnp.concatenate([x[cubes - s - 1] for x in blocks], 0)
            start = (s - 1) * wide + side * half
            grad_nb = grad_nb + dot(rest[:, start : start + half], block, ((1,), (1,)))
    flat_b = (near_b.astype(f32) - mean_bn) * inv_bn
    stats_b = jnp.stack([jnp.sum(grad_nb, axis=0), jnp.sum(grad_nb * flat_b, axis=0)])
    stats_a, stats_b, grad_nb = together((stats_a, stats_b, grad_nb))
    for bit in (2, 4):
        stats_a = stats_a + swap_k(stats_a, bit)
    for mask in [1] + h_masks:
        stats_b = stats_b + swap(stats_b, mask)
    stats_a, stats_b = together((stats_a, stats_b))
    loss = stats_a[2, 0]
    stats_a, stats_b = stats_a / count, stats_b / count

    flat_a = (all_a.astype(f32) - mean_ah) * inv_ah
    out_a = (inv_ah * (cross - stats_a[0:1] - flat_a * stats_a[1:2])).astype(bf16)
    mine = cubes * rows
    both = jnp.concatenate([out_a[:mine], swap(out_a[mine:], 1)], 1)
    both, stats_b, grad_nb = together((both, stats_b, grad_nb))
    blocks = [both[s * rows : (s + 1) * rows] for s in range(cubes)]
    blocks = [blocks[0]] + [turn(blocks[s], -s) for s in range(1, cubes)]
    grad_a = place(blocks, jnp.stack(at))
    out_b = exchange(finish(grad_nb, near_b, mean_bn, inv_bn, stats_b[0:1], stats_b[1:2], k))
    grad_b = jnp.concatenate([out_b[r] for r in range(cube)], 1)
    return (loss, grad_a, grad_b)


def solution(mesh):
    return jax.shard_map(
        shards,
        mesh=mesh,
        in_specs=(P("dp", None), P("dp", None)),
        out_specs=(P(), P("dp", None), P("dp", None)),
        check_vma=False,
    )
```

```python
import functools
import math

import jax
import jax.numpy as jnp
from jax import lax
from jax.experimental import pallas as pl
from jax.experimental.pallas import tpu as pltpu
from jax.sharding import PartitionSpec as P

lam = 0.0051
eps = 1e-05

cube = 8
orders = ((4, 2, 1), (1, 4, 2), (2, 1, 4))
together = lax.optimization_barrier
vmem = pl.BlockSpec(memory_space=pltpu.VMEM)
smem = pl.BlockSpec(memory_space=pltpu.SMEM)


def room(*arrays):
    sizes = [math.prod(x.shape) * x.dtype.itemsize for x in arrays]
    return pltpu.CompilerParams(vmem_limit_bytes=sum(sizes) + max(sizes) + (4 << 20))


def places(order):
    return [
        sum(bit for step, bit in enumerate(order) if place >> step & 1) for place in range(cube)
    ]


def cuts(width):
    part = -(-width // 384) * 128
    edges = list(range(0, width, part)) + [width]
    return list(zip(edges, edges[1:]))


def prepare_kernel(half, at_ref, a_ref, b_ref, *outs):
    near_ref, rest_ref, eighths_ref, sums_ref = outs[:4]
    rows, width = a_ref.shape
    for n in range(width // half):
        column = a_ref[:, pl.ds(pl.multiple_of(at_ref[n] * half, half), half)]
        if n < 2:
            near_ref[:, n * half : (n + 1) * half] = column
        else:
            rest_ref[:, (n - 2) * half : (n - 1) * half] = column
    parts = iter(outs[4:])
    for full_ref in (near_ref, rest_ref):
        for lo, hi in cuts(full_ref.shape[1]):
            next(parts)[...] = full_ref[:, lo:hi]
    narrow = width // cube
    for i in range(cube):
        here = slice(i * narrow, (i + 1) * narrow)
        eighths_ref[i] = b_ref[:, here]
        for n, ref in enumerate((a_ref, b_ref)):
            x = ref[:, here].astype(jnp.float32)
            sums_ref[2 * n : 2 * n + 1, here] = jnp.sum(x, axis=0, keepdims=True)
            sums_ref[2 * n + 1 : 2 * n + 2, here] = jnp.sum(x * x, axis=0, keepdims=True)


def prepare(view_a, view_b, at, half):
    rows, width = view_a.shape
    widths = [2 * half, width - 2 * half]
    shapes = [(rows, n) for n in widths] + [(cube, rows, width // cube)]
    parts = [(rows, hi - lo) for n in widths for lo, hi in cuts(n)]
    outs = [jax.ShapeDtypeStruct(shape, jnp.bfloat16) for shape in shapes]
    outs += [jax.ShapeDtypeStruct((4, width), jnp.float32)]
    outs += [jax.ShapeDtypeStruct(shape, jnp.bfloat16) for shape in parts]
    near, rest, eighths, sums, *parts = pl.pallas_call(
        functools.partial(prepare_kernel, half),
        out_shape=outs,
        in_specs=[smem, vmem, vmem],
        out_specs=[vmem] * len(outs),
        compiler_params=room(view_a, view_b, *outs),
    )(at, view_a, view_b)
    first = len(cuts(widths[0]))
    return near, rest, eighths, sums, parts[:first], parts[first:]


def double_kernel(*refs):
    n = len(refs) // 3
    for x, y, out in zip(refs[:n], refs[n : 2 * n], refs[2 * n :]):
        rows = x.shape[0]
        out[:rows, :] = x[...]
        out[rows:, :] = y[...]


def double(xs, ys):
    return pl.pallas_call(
        double_kernel,
        out_shape=[jax.ShapeDtypeStruct((2 * x.shape[0], x.shape[1]), x.dtype) for x in xs],
        in_specs=[vmem] * (2 * len(xs)),
        out_specs=[vmem] * len(xs),
        compiler_params=room(*xs, *ys, *xs, *ys),
    )(*xs, *ys)


def merge_kernel(orders, mean_ref, inv_ref, *refs):
    pieces, out_ref = refs[:-1], refs[-1]
    rows = pieces[0].shape[0] * 2 // cube
    start = 0
    for n, order in enumerate(orders[: len(pieces) // 2]):
        size = pieces[2 * n].shape[1]
        mean, inv = mean_ref[:, start : start + size], inv_ref[:, start : start + size]
        for m, r in enumerate(places(order)):
            piece, first = pieces[2 * n + 2 * m // cube], m % (cube // 2) * rows
            raw = piece[first : first + rows, :].astype(jnp.float32)
            out_ref[r * rows : (r + 1) * rows, start : start + size] = (
                (raw - mean) * inv
            ).astype(jnp.bfloat16)
        start += size


def merge(moving, arrived, orders, mean, inv):
    pieces = [x for pair in zip(moving, arrived) for x in pair]
    return pl.pallas_call(
        functools.partial(merge_kernel, orders),
        out_shape=jax.ShapeDtypeStruct((2 * pieces[0].shape[0], mean.shape[1]), jnp.bfloat16),
        in_specs=[vmem] * (2 + len(pieces)),
        out_specs=vmem,
        compiler_params=room(*pieces, *pieces),
    )(mean, inv, *pieces)


def moments_kernel(orders, mean_ref, inv_ref, *refs):
    pieces, out_ref = refs[:-1], refs[-1]
    rows = pieces[0].shape[0] * 2 // cube
    start = 0
    for n in range(len(pieces) // 2):
        size = pieces[2 * n].shape[1]
        here = slice(start, start + size)
        mean, inv = mean_ref[:, here], inv_ref[:, here]
        total = [jnp.zeros((1, size), jnp.float32)] * 4
        for piece in pieces[2 * n : 2 * n + 2]:
            for m in range(cube // 2):
                raw = piece[m * rows : (m + 1) * rows, :].astype(jnp.float32)
                flat = (raw - mean) * inv
                norm = flat.astype(jnp.bfloat16).astype(jnp.float32)
                terms = (flat, flat * norm, norm * norm, norm)
                total = [t + jnp.sum(x, axis=0, keepdims=True) for t, x in zip(total, terms)]
        out_ref[:, here] = jnp.concatenate(total, 0)
        start += size


def moments(moving, arrived, orders, mean, inv):
    pieces = [x for pair in zip(moving, arrived) for x in pair]
    return pl.pallas_call(
        functools.partial(moments_kernel, orders),
        out_shape=jax.ShapeDtypeStruct((4, mean.shape[1]), jnp.float32),
        in_specs=[vmem] * (2 + len(pieces)),
        out_specs=vmem,
        compiler_params=room(*pieces),
    )(mean, inv, *pieces)


def arrange_kernel(k_ref, blocks_ref, mean_ref, inv_ref, raw_ref, norm_ref):
    rows = blocks_ref.shape[1]
    for r in range(cube):
        raw = blocks_ref[k_ref[0] ^ r]
        raw_ref[r * rows : (r + 1) * rows, :] = raw
        norm_ref[r * rows : (r + 1) * rows, :] = (
            (raw.astype(jnp.float32) - mean_ref[...]) * inv_ref[...]
        ).astype(jnp.bfloat16)


def arrange(blocks, mean, inv, k):
    _, rows, n = blocks.shape
    out = jax.ShapeDtypeStruct((cube * rows, n), jnp.bfloat16)
    return pl.pallas_call(
        arrange_kernel,
        out_shape=(out, out),
        in_specs=[smem] + [vmem] * 3,
        out_specs=(vmem, vmem),
        compiler_params=room(blocks, out, out),
    )(k.reshape(1), blocks, mean, inv)


def finish_kernel(k_ref, grad_ref, raw_ref, mean_ref, inv_ref, first_ref, second_ref, out_ref):
    rows = out_ref.shape[1]
    mean, inv = mean_ref[...], inv_ref[...]
    for r in range(cube):
        here = slice(r * rows, (r + 1) * rows)
        flat = (raw_ref[here, :].astype(jnp.float32) - mean) * inv
        out = inv * (grad_ref[here, :] - first_ref[...] - flat * second_ref[...])
        out_ref[k_ref[0] ^ r] = out.astype(jnp.bfloat16)


def finish(grad, raw, mean, inv, first, second, k):
    size, n = grad.shape
    return pl.pallas_call(
        finish_kernel,
        out_shape=jax.ShapeDtypeStruct((cube, size // cube, n), jnp.bfloat16),
        in_specs=[smem] + [vmem] * 6,
        out_specs=vmem,
        compiler_params=room(grad, raw, raw),
    )(k.reshape(1), grad, raw, mean, inv, first, second)


def place_kernel(at_ref, *refs):
    blocks, out_ref = refs[:-1], refs[-1]
    half = blocks[0].shape[1] // 2
    for n, block in enumerate(blocks):
        for side in range(2):
            start = pl.multiple_of(at_ref[2 * n + side] * half, half)
            out_ref[:, pl.ds(start, half)] = block[:, side * half : (side + 1) * half]


def place(blocks, at):
    rows, n = blocks[0].shape
    return pl.pallas_call(
        place_kernel,
        out_shape=jax.ShapeDtypeStruct((rows, n * len(blocks)), jnp.bfloat16),
        in_specs=[smem] + [vmem] * len(blocks),
        out_specs=vmem,
        compiler_params=room(*blocks, *blocks),
    )(at, *blocks)


def dot(x, y, contract):
    return lax.dot_general(x, y, (contract, ((), ())), preferred_element_type=jnp.float32)


def cross_kernel(side, orders, k_ref, rows_ref, *refs):
    if side == 0:
        pieces, out_ref = refs[:-1], refs[-1]
    else:
        total_ref, raw_ref, mean_ref, inv_ref, first_ref, second_ref, *pieces, out_ref = refs
    narrow = rows_ref.shape[1] // cube
    start = 0
    for order, piece in zip(orders, pieces):
        here = slice(start, start + piece.shape[1])
        start += piece.shape[1]
        total = 0.0 if side == 0 else total_ref[:, here]
        for m in range(cube // 2):
            r = places(order)[side * cube // 2 + m]
            at = pl.multiple_of((k_ref[0] ^ r) * narrow, narrow)
            total = total + jnp.dot(
                rows_ref[:, pl.ds(at, narrow)],
                piece[m * narrow : (m + 1) * narrow, :],
                preferred_element_type=jnp.float32,
            )
        if side == 0:
            out_ref[:, here] = total
        else:
            inv = inv_ref[:, here]
            flat = (raw_ref[:, here].astype(jnp.float32) - mean_ref[:, here]) * inv
            out = inv * (total - first_ref[:, here] - flat * second_ref[:, here])
            out_ref[:, here] = out.astype(jnp.bfloat16)


def cross_products(side, rows, pieces, orders, k, *more):
    size, n = rows.shape[0], sum(x.shape[1] for x in pieces)
    block = min(size, 512)

    def whole(x):
        return pl.BlockSpec(x.shape, lambda i: (0, 0))

    def part(x):
        return pl.BlockSpec((block, x.shape[1]), lambda i: (i, 0))

    out = jax.ShapeDtypeStruct((size, n), jnp.bfloat16 if side else jnp.float32)
    specs = [part(x) if x.shape[0] == size else whole(x) for x in more]
    return pl.pallas_call(
        functools.partial(cross_kernel, side, orders),
        grid=(size // block,),
        out_shape=out,
        in_specs=[smem, part(rows)] + specs + [whole(x) for x in pieces],
        out_specs=part(out),
        cost_estimate=pl.CostEstimate(
            flops=size * n * rows.shape[1], bytes_accessed=16 * size * n, transcendentals=0
        ),
        compiler_params=pltpu.CompilerParams(vmem_limit_bytes=48 << 20),
    )(k.reshape(1), rows, *more, *pieces)


def shards(view_a, view_b):
    f32, bf16 = jnp.float32, jnp.bfloat16
    rows, width = view_a.shape
    devices = lax.axis_size("dp")
    count = rows * devices
    cubes = devices // (2 * cube)
    index = lax.axis_index("dp")
    c, k, h = index % 2, index // 2 % cube, index // (2 * cube)
    wide, half, narrow = width // cubes, width // cubes // 2, width // cube
    groups = [
        [(g * cube + i) * 2 + core for i in range(cube)] for g in range(cubes) for core in range(2)
    ]

    def swap(x, mask):
        return lax.ppermute(x, "dp", [(i, i ^ mask) for i in range(devices)])

    def swap_k(x, bit):
        return swap(x, 2 * bit)

    def turn(x, step):
        return lax.ppermute(
            x, "dp", [(i, (i + 2 * cube * step) % devices) for i in range(devices)]
        )

    def turns(x):
        return [turn(x, s) for s in range(1, cubes)]

    def exchange(x):
        return lax.all_to_all(
            x, "dp", split_axis=0, concat_axis=0, axis_index_groups=groups, tiled=True
        )

    def columns(x, start, size):
        return lax.dynamic_slice_in_dim(x, start, size, axis=1)

    at = [(h + s) % cubes * 2 + core for s in range(cubes) for core in (c, 1 - c)]

    h_masks = [2 * cube << bit for bit in range(cubes.bit_length() - 1)]

    def by_place(x, sides):
        return jnp.concatenate([columns(x, place * half, half) for place in sides], 1)

    def send(moving, step):
        return [swap_k(x, order[step]) for x, order in zip(moving, orders)]

    whole_near, whole_rest, eighths, sums, near, rest = prepare(view_a, view_b, jnp.stack(at), half)
    parts_a = [whole_near] + [whole_rest[:, s * wide : (s + 1) * wide] for s in range(cubes - 1)]
    cuts_b = (0, rows // 2, rows)
    pieces_b = [view_b[lo:hi] for lo, hi in zip(cuts_b, cuts_b[1:])]
    others_b = []

    arrived = send(rest, 0)

    own_b = exchange(eighths)
    far_1 = [turn(x[:, half:], s + 1) for s, x in enumerate(parts_a[1:])]
    for mask in [1] + h_masks:
        sums = sums + swap(sums, mask)
    rest, arrived, sums, pieces_b, near, parts_a, far_1 = together(
        (rest, arrived, sums, pieces_b, near, parts_a, far_1)
    )
    rest = double(rest, arrived)
    arrived = send(rest, 1)
    others_b.append(turns(pieces_b[0]))
    for mask in (2, 4):
        sums = sums + swap(sums, mask)
    rest, arrived, others_b, sums, pieces_b, own_b, parts_a, far_1 = together(
        (rest, arrived, others_b, sums, pieces_b, own_b, parts_a, far_1)
    )
    rest = double(rest, arrived)
    arrived = send(rest, 2)
    others_b.append(turns(pieces_b[1]))
    sums = sums + swap(sums, 8)
    means = sums / count
    mean_a, mean_b = means[0:1], means[2:3]
    inv_a = 1.0 / jnp.sqrt(means[1:2] - mean_a * mean_a + eps)
    inv_b = 1.0 / jnp.sqrt(means[3:4] - mean_b * mean_b + eps)
    mean_bn = columns(mean_b, k * narrow, narrow)
    inv_bn = columns(inv_b, k * narrow, narrow)
    mean_ap, inv_ap = by_place(mean_a, at), by_place(inv_a, at)
    near_b, right = arrange(own_b, mean_bn, inv_bn, k)
    rest, arrived, others_b, near_b, right, mean_ap, inv_ap, parts_a, far_1 = together(
        (rest, arrived, others_b, near_b, right, mean_ap, inv_ap, parts_a, far_1)
    )

    def product(left, s):
        first = dot(right, left[:, s * wide + half : (s + 1) * wide], ((0,), (0,)))
        return swap(first, 1) + dot(right, left[:, s * wide : s * wide + half], ((0,), (0,)))

    def diagonal(s):
        return (
            lax.broadcasted_iota(jnp.int32, (narrow, half), 1) + at[2 * s] * half
            == lax.broadcasted_iota(jnp.int32, (narrow, half), 0) + k * narrow
        )

    raw_rest = (rest, arrived)
    rest = merge(rest, arrived, orders, mean_ap[:, wide:], inv_ap[:, wide:])
    arrived = send(near, 0)
    partials = [product(rest, s) for s in range(cubes - 1)]
    exact = [
        jnp.sum(jnp.where(diagonal(s + 1), x, 0.0), axis=1).reshape(1, narrow)
        for s, x in enumerate(partials)
    ]
    partials = [x.astype(bf16) for x in partials]
    partials, exact, near, arrived, others_b, raw_rest, near_b = together(
        (partials, exact, near, arrived, others_b, raw_rest, near_b)
    )
    near = double(near, arrived)

    cuts_p = (0, 3 * narrow // 8, 7 * narrow // 8, narrow)
    received = []
    for step in (1, 2):
        arrived = send(near, step)
        received.append(
            [turn(x[cuts_p[step - 1] : cuts_p[step]], s + 1) for s, x in enumerate(partials)]
        )
        if step == 1:
            other_a = swap(jnp.concatenate([parts_a[0][:, half:]] + far_1, 0), 1)
            flat_b = (near_b.astype(f32) - mean_bn) * inv_bn
            wide_b = flat_b.astype(bf16).astype(f32)
            sums_b = jnp.stack(
                [jnp.sum(x, axis=0) for x in (flat_b, flat_b * wide_b, wide_b * wide_b, wide_b)]
            )
            sums_b = sums_b + swap(sums_b, 1)
            sums_a = moments(*raw_rest, orders, mean_ap[:, wide:], inv_ap[:, wide:])
            near, arrived, received, partials, exact, others_b, other_a, sums_a, sums_b = together(
                (near, arrived, received, partials, exact, others_b, other_a, sums_a, sums_b)
            )
            near = double(near, arrived)
        else:
            others_b = [jnp.concatenate(pieces, 0) for pieces in zip(*others_b)]
            pair_b = jnp.concatenate([view_b] + others_b, 0)
            pair_b = ((pair_b.astype(f32) - mean_b) * inv_b).astype(bf16)
            far_sums = [
                turn(jnp.concatenate([sums_a[:, s * wide : (s + 1) * wide], sums_b], 1), s + 1)
                for s in range(cubes - 1)
            ]
            near, arrived, received, partials, exact, pair_b, far_sums = together(
                (near, arrived, received, partials, exact, pair_b, far_sums)
            )
            sums_a = sum(x[:, :wide] for x in far_sums)
            sums_b = sums_b + sum(x[:, wide:] for x in far_sums)
    received.append([turn(x[cuts_p[2] :], s + 1) for s, x in enumerate(partials)])
    exact = [turn(x, s + 1) for s, x in enumerate(exact)]
    raw_near = (near, arrived)
    near = merge(near, arrived, orders, mean_ap[:, :wide], inv_ap[:, :wide])
    norm_b = jnp.concatenate([pair_b, swap(pair_b, 1)], 0)
    corr = product(near, 0)
    corr, received, exact, norm_b, raw_near = together(
        (corr, received, exact, norm_b, raw_near)
    )
    diag = diagonal(0)
    for blocks, line in zip(zip(*received), exact):
        block = jnp.concatenate(blocks, 0).astype(f32)
        corr = corr + jnp.where(diag, line.reshape(narrow, 1), block)
    corr = corr / count
    loss = jnp.sum(jnp.where(diag, (1.0 - corr) ** 2, lam * corr * corr))
    gcorr = jnp.where(diag, 2.0 * (corr - 1.0), 2.0 * lam * corr).astype(bf16)

    def line(sums):
        spread = sums[2:3] - sums[3:4] * sums[3:4] / count
        usable = spread > 1e-3 * sums[2:3]
        slope = jnp.where(
            usable,
            (sums[1:2] - sums[0:1] * sums[3:4] / count) / jnp.where(usable, spread, 1.0),
            1.0,
        )
        return slope, (sums[0:1] - slope * sums[3:4]) / count

    stats_a = jnp.stack(
        [
            jnp.sum(gcorr.astype(f32) * sums_b[3].reshape(narrow, 1), axis=0),
            jnp.sum(gcorr.astype(f32) * corr, axis=0),
            jnp.full((half,), loss),
        ]
    )

    moving = [gcorr[:, lo:hi] for lo, hi in cuts(half)]
    cuts_g = (0, 3 * narrow // 8, 3 * narrow // 4, narrow)
    mean_ah, inv_ah = mean_ap[:, :half], inv_ap[:, :half]
    turned, sibling = [], []
    for step in range(3):
        arrived = send(moving, step)
        piece = gcorr[cuts_g[step] : cuts_g[step + 1]]
        if step < 2:
            turned.append(turns(piece))
        else:
            both = [
                turn(jnp.concatenate([piece, x[:, :half]], 0), s + 1)
                for s, x in enumerate(parts_a[1:])
            ]
            turned.append([x[: narrow // 4] for x in both])
            far_0 = [x[narrow // 4 :] for x in both]
        if step == 0:
            for bit in (1, 2):
                stats_a = stats_a + swap_k(stats_a, bit)
            sums_a = sums_a + moments(*raw_near, orders, mean_ap[:, :wide], inv_ap[:, :wide])
            moving, arrived, turned, gcorr, parts_a, stats_a, sums_a, corr = together(
                (moving, arrived, turned, gcorr, parts_a, stats_a, sums_a, corr)
            )
        elif step == 1:
            sums_a = sums_a[:, :half] + swap(sums_a[:, half:], 1)
            both_g = jnp.sum(gcorr.astype(f32) * corr, axis=1)
            near_block = [swap(jnp.concatenate([gcorr] + turned[0], 0), 1)]
            sibling.append(
                [
                    near_block[0][narrow + s * cuts_g[1] : narrow + (s + 1) * cuts_g[1]]
                    for s in range(cubes - 1)
                ]
            )
            own = jnp.concatenate([gcorr, near_block[0][:narrow]], 1)
            moving, arrived, turned, gcorr, sibling, parts_a, own, stats_a, sums_a, both_g = together(
                (moving, arrived, turned, gcorr, sibling, parts_a, own, stats_a, sums_a, both_g)
            )
        else:
            cross = cross_products(0, norm_b, moving, orders, k)
            grad_nb = dot(near, own, ((1,), (1,)))
            stats_b = jnp.stack([jnp.sum(gcorr.astype(f32) * sums_a[3:4], axis=1), both_g])
            stats_a = stats_a + swap_k(stats_a, 4)
            line_a, line_b = line(sums_a), line(sums_b)
            (
                arrived, turned, sibling, far_0, cross, mean_ah, inv_ah, grad_nb, stats_a, stats_b,
                line_a, line_b,
            ) = together(
                (
                    arrived, turned, sibling, far_0, cross, mean_ah, inv_ah, grad_nb, stats_a,
                    stats_b, line_a, line_b,
                )
            )
        if step < 2:
            moving = double(moving, arrived)

    for step in (1, 2):
        sibling.append([swap(x, 1) for x in turned[step]])
    loss = jnp.broadcast_to(stats_a[2:3, :128], (8, 128))
    first_a = stats_a[0:1] / count
    second_a = line_a[0] * stats_a[1:2] + line_a[1] * first_a
    all_a = jnp.concatenate([parts_a[0][:, :half]] + far_0 + [other_a], 0)
    out_a = cross_products(
        1, norm_b, arrived, orders, k, cross, all_a, mean_ah, inv_ah, first_a, second_a
    )
    out_a, stats_b, sibling, rest, loss = together((out_a, stats_b, sibling, rest, loss))
    for mask in h_masks:
        stats_b = stats_b + swap(stats_b, mask)

    for s in range(1, cubes):
        for side, blocks in enumerate((turned, sibling)):
            block = jnp.concatenate([x[cubes - s - 1] for x in blocks], 0)
            start = (s - 1) * wide + side * half
            grad_nb = grad_nb + dot(rest[:, start : start + half], block, ((1,), (1,)))

    mine = cubes * rows
    both = jnp.concatenate([out_a[:mine], swap(out_a[mine:], 1)], 1)
    both, grad_nb, loss, stats_b = together((both, grad_nb, loss, stats_b))
    stats_b = stats_b + swap(stats_b, 1)
    loss = loss + swap(loss, 1)
    first_b = stats_b[0:1] / count
    second_b = line_b[0] * stats_b[1:2] + line_b[1] * first_b
    for mask in h_masks:
        loss = loss + swap(loss, mask)
    blocks = [both[s * rows : (s + 1) * rows] for s in range(cubes)]
    blocks = [blocks[0]] + [turn(blocks[s], -s) for s in range(1, cubes)]
    grad_a = place(blocks, jnp.stack(at))
    out_b = exchange(finish(grad_nb, near_b, mean_bn, inv_bn, first_b, second_b, k))
    grad_b = jnp.concatenate([out_b[r] for r in range(cube)], 1)
    return (loss[0, 0], grad_a, grad_b)


def solution(mesh):
    return jax.shard_map(
        shards,
        mesh=mesh,
        in_specs=(P("dp", None), P("dp", None)),
        out_specs=(P(), P("dp", None), P("dp", None)),
        check_vma=False,
    )
```

```python
import functools
import math

import jax
import jax.numpy as jnp
from jax import lax
from jax.experimental import pallas as pl
from jax.experimental.pallas import tpu as pltpu
from jax.sharding import PartitionSpec as P

lam = 0.0051
eps = 1e-05

cube = 8
orders = ((4, 2, 1), (1, 4, 2), (2, 1, 4))
together = lax.optimization_barrier
strip = 32
vmem = pl.BlockSpec(memory_space=pltpu.VMEM)
smem = pl.BlockSpec(memory_space=pltpu.SMEM)


def room(*arrays):
    sizes = [math.prod(x.shape) * x.dtype.itemsize for x in arrays]
    return pltpu.CompilerParams(vmem_limit_bytes=sum(sizes) + max(sizes) + (4 << 20))


def strips(rows, body, init=None):
    return lax.fori_loop(
        0, rows // strip, lambda i, carry: body(pl.multiple_of(i * strip, strip), carry), init
    )


def places(order):
    return [
        sum(bit for step, bit in enumerate(order) if place >> step & 1) for place in range(cube)
    ]


def cuts(width):
    part = -(-width // 384) * 128
    edges = list(range(0, width, part)) + [width]
    return list(zip(edges, edges[1:]))


def prepare_kernel(half, at_ref, a_ref, b_ref, *outs):
    near_ref, rest_ref, eighths_ref, sums_ref = outs[:4]
    rows, width = a_ref.shape
    for n in range(width // half):
        column = a_ref[:, pl.ds(pl.multiple_of(at_ref[n] * half, half), half)]
        if n < 2:
            near_ref[:, n * half : (n + 1) * half] = column
        else:
            rest_ref[:, (n - 2) * half : (n - 1) * half] = column
    parts = iter(outs[4:])
    for full_ref in (near_ref, rest_ref):
        for lo, hi in cuts(full_ref.shape[1]):
            next(parts)[...] = full_ref[:, lo:hi]
    narrow = width // cube
    for i in range(cube):
        here = slice(i * narrow, (i + 1) * narrow)
        eighths_ref[i] = b_ref[:, here]
        for n, ref in enumerate((a_ref, b_ref)):
            x = ref[:, here].astype(jnp.float32)
            sums_ref[2 * n : 2 * n + 1, here] = jnp.sum(x, axis=0, keepdims=True)
            sums_ref[2 * n + 1 : 2 * n + 2, here] = jnp.sum(x * x, axis=0, keepdims=True)


def prepare(view_a, view_b, at, half):
    rows, width = view_a.shape
    widths = [2 * half, width - 2 * half]
    shapes = [(rows, n) for n in widths] + [(cube, rows, width // cube)]
    parts = [(rows, hi - lo) for n in widths for lo, hi in cuts(n)]
    outs = [jax.ShapeDtypeStruct(shape, jnp.bfloat16) for shape in shapes]
    outs += [jax.ShapeDtypeStruct((4, width), jnp.float32)]
    outs += [jax.ShapeDtypeStruct(shape, jnp.bfloat16) for shape in parts]
    near, rest, eighths, sums, *parts = pl.pallas_call(
        functools.partial(prepare_kernel, half),
        out_shape=outs,
        in_specs=[smem, vmem, vmem],
        out_specs=[vmem] * len(outs),
        compiler_params=room(view_a, view_b, *outs),
    )(at, view_a, view_b)
    first = len(cuts(widths[0]))
    return near, rest, eighths, sums, parts[:first], parts[first:]


def double_kernel(*refs):
    n = len(refs) // 3
    for x, y, out in zip(refs[:n], refs[n : 2 * n], refs[2 * n :]):
        rows = x.shape[0]

        def body(row, _, x=x, y=y, out=out, rows=rows):
            out[pl.ds(row, strip), :] = x[pl.ds(row, strip), :]
            out[pl.ds(rows + row, strip), :] = y[pl.ds(row, strip), :]

        strips(rows, body)


def double(xs, ys):
    return pl.pallas_call(
        double_kernel,
        out_shape=[jax.ShapeDtypeStruct((2 * x.shape[0], x.shape[1]), x.dtype) for x in xs],
        in_specs=[vmem] * (2 * len(xs)),
        out_specs=[vmem] * len(xs),
        compiler_params=room(*xs, *ys, *xs, *ys),
    )(*xs, *ys)


def merge_kernel(orders, mean_ref, inv_ref, *refs):
    pieces, out_ref = refs[:-1], refs[-1]
    rows = pieces[0].shape[0] * 2 // cube
    start = 0
    for n, order in enumerate(orders[: len(pieces) // 2]):
        size = pieces[2 * n].shape[1]
        mean, inv = mean_ref[:, start : start + size], inv_ref[:, start : start + size]
        for m, r in enumerate(places(order)):
            piece, first = pieces[2 * n + 2 * m // cube], m % (cube // 2) * rows


            def body(row, _, piece=piece, first=first, r=r, start=start, size=size, mean=mean, inv=inv):
                raw = piece[pl.ds(first + row, strip), :].astype(jnp.float32)
                out_ref[pl.ds(r * rows + row, strip), start : start + size] = (
                    (raw - mean) * inv
                ).astype(jnp.bfloat16)

            strips(rows, body)
        start += size


def merge(moving, arrived, orders, mean, inv):
    pieces = [x for pair in zip(moving, arrived) for x in pair]
    return pl.pallas_call(
        functools.partial(merge_kernel, orders),
        out_shape=jax.ShapeDtypeStruct((2 * pieces[0].shape[0], mean.shape[1]), jnp.bfloat16),
        in_specs=[vmem] * (2 + len(pieces)),
        out_specs=vmem,
        compiler_params=room(*pieces, *pieces),
    )(mean, inv, *pieces)


def moments_kernel(orders, mean_ref, inv_ref, *refs):
    pieces, out_ref = refs[:-1], refs[-1]
    start = 0
    for n in range(len(pieces) // 2):
        size = pieces[2 * n].shape[1]
        here = slice(start, start + size)
        mean, inv = mean_ref[:, here], inv_ref[:, here]
        total = [jnp.zeros((8, size), jnp.float32)] * 4
        for piece in pieces[2 * n : 2 * n + 2]:

            def body(row, total, piece=piece, mean=mean, inv=inv):
                raw = piece[pl.ds(row, strip), :].astype(jnp.float32)
                flat = (raw - mean) * inv
                norm = flat.astype(jnp.bfloat16).astype(jnp.float32)
                terms = (flat, flat * norm, norm * norm, norm)
                return [
                    t + sum(x[m : m + 8, :] for m in range(0, strip, 8))
                    for t, x in zip(total, terms)
                ]

            total = strips(piece.shape[0], body, total)
        total = [jnp.sum(x, axis=0, keepdims=True) for x in total]
        out_ref[:, here] = jnp.concatenate(total, 0)
        start += size


def moments(moving, arrived, orders, mean, inv):
    pieces = [x for pair in zip(moving, arrived) for x in pair]
    return pl.pallas_call(
        functools.partial(moments_kernel, orders),
        out_shape=jax.ShapeDtypeStruct((4, mean.shape[1]), jnp.float32),
        in_specs=[vmem] * (2 + len(pieces)),
        out_specs=vmem,
        compiler_params=room(*pieces),
    )(mean, inv, *pieces)


def arrange_kernel(k_ref, blocks_ref, mean_ref, inv_ref, raw_ref, norm_ref):
    rows = blocks_ref.shape[1]
    for r in range(cube):

        def body(row, _, r=r):
            raw = blocks_ref[k_ref[0] ^ r, pl.ds(row, strip), :]
            raw_ref[pl.ds(r * rows + row, strip), :] = raw
            norm_ref[pl.ds(r * rows + row, strip), :] = (
                (raw.astype(jnp.float32) - mean_ref[...]) * inv_ref[...]
            ).astype(jnp.bfloat16)

        strips(rows, body)


def arrange(blocks, mean, inv, k):
    _, rows, n = blocks.shape
    out = jax.ShapeDtypeStruct((cube * rows, n), jnp.bfloat16)
    return pl.pallas_call(
        arrange_kernel,
        out_shape=(out, out),
        in_specs=[smem] + [vmem] * 3,
        out_specs=(vmem, vmem),
        compiler_params=room(blocks, out, out),
    )(k.reshape(1), blocks, mean, inv)


def finish_kernel(k_ref, grad_ref, raw_ref, mean_ref, inv_ref, first_ref, second_ref, out_ref):
    rows = out_ref.shape[1]
    mean, inv = mean_ref[...], inv_ref[...]
    for r in range(cube):

        def body(row, _, r=r):
            here = pl.ds(r * rows + row, strip)
            flat = (raw_ref[here, :].astype(jnp.float32) - mean) * inv
            out = inv * (grad_ref[here, :] - first_ref[...] - flat * second_ref[...])
            out_ref[k_ref[0] ^ r, pl.ds(row, strip), :] = out.astype(jnp.bfloat16)

        strips(rows, body)


def finish(grad, raw, mean, inv, first, second, k):
    size, n = grad.shape
    return pl.pallas_call(
        finish_kernel,
        out_shape=jax.ShapeDtypeStruct((cube, size // cube, n), jnp.bfloat16),
        in_specs=[smem] + [vmem] * 6,
        out_specs=vmem,
        compiler_params=room(grad, raw, raw),
    )(k.reshape(1), grad, raw, mean, inv, first, second)


def place_kernel(at_ref, *refs):
    blocks, out_ref = refs[:-1], refs[-1]
    half = blocks[0].shape[1] // 2
    for n, block in enumerate(blocks):
        for side in range(2):
            start = pl.multiple_of(at_ref[2 * n + side] * half, half)
            out_ref[:, pl.ds(start, half)] = block[:, side * half : (side + 1) * half]


def place(blocks, at):
    rows, n = blocks[0].shape
    return pl.pallas_call(
        place_kernel,
        out_shape=jax.ShapeDtypeStruct((rows, n * len(blocks)), jnp.bfloat16),
        in_specs=[smem] + [vmem] * len(blocks),
        out_specs=vmem,
        compiler_params=room(*blocks, *blocks),
    )(at, *blocks)


def dot(x, y, contract):
    return lax.dot_general(x, y, (contract, ((), ())), preferred_element_type=jnp.float32)


def cross_kernel(side, orders, k_ref, rows_ref, *refs):
    if side == 0:
        pieces, out_ref = refs[:-1], refs[-1]
    else:
        total_ref, raw_ref, mean_ref, inv_ref, first_ref, second_ref, *pieces, out_ref = refs
    narrow = rows_ref.shape[1] // cube
    start = 0
    for order, piece in zip(orders, pieces):
        here = slice(start, start + piece.shape[1])
        start += piece.shape[1]
        total = 0.0 if side == 0 else total_ref[:, here]
        for m in range(cube // 2):
            r = places(order)[side * cube // 2 + m]
            at = pl.multiple_of((k_ref[0] ^ r) * narrow, narrow)
            total = total + jnp.dot(
                rows_ref[:, pl.ds(at, narrow)],
                piece[m * narrow : (m + 1) * narrow, :],
                preferred_element_type=jnp.float32,
            )
        if side == 0:
            out_ref[:, here] = total
        else:
            inv = inv_ref[:, here]
            flat = (raw_ref[:, here].astype(jnp.float32) - mean_ref[:, here]) * inv
            out = inv * (total - first_ref[:, here] - flat * second_ref[:, here])
            out_ref[:, here] = out.astype(jnp.bfloat16)


def cross_products(side, rows, pieces, orders, k, *more):
    size, n = rows.shape[0], sum(x.shape[1] for x in pieces)
    block = min(size, 512)

    def whole(x):
        return pl.BlockSpec(x.shape, lambda i: (0, 0))

    def part(x):
        return pl.BlockSpec((block, x.shape[1]), lambda i: (i, 0))

    out = jax.ShapeDtypeStruct((size, n), jnp.bfloat16 if side else jnp.float32)
    specs = [part(x) if x.shape[0] == size else whole(x) for x in more]
    return pl.pallas_call(
        functools.partial(cross_kernel, side, orders),
        grid=(size // block,),
        out_shape=out,
        in_specs=[smem, part(rows)] + specs + [whole(x) for x in pieces],
        out_specs=part(out),
        cost_estimate=pl.CostEstimate(
            flops=size * n * rows.shape[1], bytes_accessed=16 * size * n, transcendentals=0
        ),
        compiler_params=pltpu.CompilerParams(vmem_limit_bytes=48 << 20),
    )(k.reshape(1), rows, *more, *pieces)


def shards(view_a, view_b):
    f32, bf16 = jnp.float32, jnp.bfloat16
    rows, width = view_a.shape
    devices = lax.axis_size("dp")
    count = rows * devices
    cubes = devices // (2 * cube)
    index = lax.axis_index("dp")
    c, k, h = index % 2, index // 2 % cube, index // (2 * cube)
    wide, half, narrow = width // cubes, width // cubes // 2, width // cube
    groups = [
        [(g * cube + i) * 2 + core for i in range(cube)] for g in range(cubes) for core in range(2)
    ]

    def swap(x, mask):
        return lax.ppermute(x, "dp", [(i, i ^ mask) for i in range(devices)])

    def swap_k(x, bit):
        return swap(x, 2 * bit)

    def turn(x, step):
        return lax.ppermute(
            x, "dp", [(i, (i + 2 * cube * step) % devices) for i in range(devices)]
        )

    def turns(x):
        return [turn(x, s) for s in range(1, cubes)]

    def exchange(x):
        return lax.all_to_all(
            x, "dp", split_axis=0, concat_axis=0, axis_index_groups=groups, tiled=True
        )

    def columns(x, start, size):
        return lax.dynamic_slice_in_dim(x, start, size, axis=1)

    at = [(h + s) % cubes * 2 + core for s in range(cubes) for core in (c, 1 - c)]

    h_masks = [2 * cube << bit for bit in range(cubes.bit_length() - 1)]

    def by_place(x, sides):
        return jnp.concatenate([columns(x, place * half, half) for place in sides], 1)

    def send(moving, step):
        return [swap_k(x, order[step]) for x, order in zip(moving, orders)]

    whole_near, whole_rest, eighths, sums, near, rest = prepare(view_a, view_b, jnp.stack(at), half)
    parts_a = [whole_near] + [whole_rest[:, s * wide : (s + 1) * wide] for s in range(cubes - 1)]
    cuts_b = (0, rows // 2, rows)
    pieces_b = [view_b[lo:hi] for lo, hi in zip(cuts_b, cuts_b[1:])]
    others_b = []

    arrived = send(rest, 0)

    own_b = exchange(eighths)
    far_1 = [turn(x[:, half:], s + 1) for s, x in enumerate(parts_a[1:])]
    for mask in [1] + h_masks:
        sums = sums + swap(sums, mask)
    rest, arrived, sums, pieces_b, near, parts_a, far_1 = together(
        (rest, arrived, sums, pieces_b, near, parts_a, far_1)
    )
    rest = double(rest, arrived)
    arrived = send(rest, 1)
    others_b.append(turns(pieces_b[0]))
    for mask in (2, 4):
        sums = sums + swap(sums, mask)
    rest, arrived, others_b, sums, pieces_b, own_b, parts_a, far_1 = together(
        (rest, arrived, others_b, sums, pieces_b, own_b, parts_a, far_1)
    )
    rest = double(rest, arrived)
    arrived = send(rest, 2)
    others_b.append(turns(pieces_b[1]))
    sums = sums + swap(sums, 8)
    means = sums / count
    mean_a, mean_b = means[0:1], means[2:3]
    inv_a = 1.0 / jnp.sqrt(means[1:2] - mean_a * mean_a + eps)
    inv_b = 1.0 / jnp.sqrt(means[3:4] - mean_b * mean_b + eps)
    mean_bn = columns(mean_b, k * narrow, narrow)
    inv_bn = columns(inv_b, k * narrow, narrow)
    mean_ap, inv_ap = by_place(mean_a, at), by_place(inv_a, at)
    near_b, right = arrange(own_b, mean_bn, inv_bn, k)
    rest, arrived, others_b, near_b, right, mean_ap, inv_ap, parts_a, far_1 = together(
        (rest, arrived, others_b, near_b, right, mean_ap, inv_ap, parts_a, far_1)
    )

    def product(left, s):
        first = dot(right, left[:, s * wide + half : (s + 1) * wide], ((0,), (0,)))
        return swap(first, 1) + dot(right, left[:, s * wide : s * wide + half], ((0,), (0,)))

    def diagonal(s):
        return (
            lax.broadcasted_iota(jnp.int32, (narrow, half), 1) + at[2 * s] * half
            == lax.broadcasted_iota(jnp.int32, (narrow, half), 0) + k * narrow
        )

    raw_rest = (rest, arrived)
    rest = merge(rest, arrived, orders, mean_ap[:, wide:], inv_ap[:, wide:])
    arrived = send(near, 0)
    partials = [product(rest, s) for s in range(cubes - 1)]
    exact = [
        jnp.sum(jnp.where(diagonal(s + 1), x, 0.0), axis=1).reshape(1, narrow)
        for s, x in enumerate(partials)
    ]
    partials = [x.astype(bf16) for x in partials]
    partials, exact, near, arrived, others_b, raw_rest, near_b = together(
        (partials, exact, near, arrived, others_b, raw_rest, near_b)
    )
    near = double(near, arrived)

    cuts_p = (0, 3 * narrow // 8, 7 * narrow // 8, narrow)
    received = []
    for step in (1, 2):
        arrived = send(near, step)
        received.append(
            [turn(x[cuts_p[step - 1] : cuts_p[step]], s + 1) for s, x in enumerate(partials)]
        )
        if step == 1:
            other_a = swap(jnp.concatenate([parts_a[0][:, half:]] + far_1, 0), 1)
            flat_b = (near_b.astype(f32) - mean_bn) * inv_bn
            wide_b = flat_b.astype(bf16).astype(f32)
            sums_b = jnp.stack(
                [jnp.sum(x, axis=0) for x in (flat_b, flat_b * wide_b, wide_b * wide_b, wide_b)]
            )
            sums_b = sums_b + swap(sums_b, 1)
            sums_a = moments(*raw_rest, orders, mean_ap[:, wide:], inv_ap[:, wide:])
            near, arrived, received, partials, exact, others_b, other_a, sums_a, sums_b = together(
                (near, arrived, received, partials, exact, others_b, other_a, sums_a, sums_b)
            )
            near = double(near, arrived)
        else:
            others_b = [jnp.concatenate(pieces, 0) for pieces in zip(*others_b)]
            pair_b = jnp.concatenate([view_b] + others_b, 0)
            pair_b = ((pair_b.astype(f32) - mean_b) * inv_b).astype(bf16)
            far_sums = [
                turn(jnp.concatenate([sums_a[:, s * wide : (s + 1) * wide], sums_b], 1), s + 1)
                for s in range(cubes - 1)
            ]
            near, arrived, received, partials, exact, pair_b, far_sums = together(
                (near, arrived, received, partials, exact, pair_b, far_sums)
            )
            sums_a = sum(x[:, :wide] for x in far_sums)
            sums_b = sums_b + sum(x[:, wide:] for x in far_sums)
    received.append([turn(x[cuts_p[2] :], s + 1) for s, x in enumerate(partials)])
    exact = [turn(x, s + 1) for s, x in enumerate(exact)]
    raw_near = (near, arrived)
    near = merge(near, arrived, orders, mean_ap[:, :wide], inv_ap[:, :wide])
    norm_b = jnp.concatenate([pair_b, swap(pair_b, 1)], 0)
    corr = product(near, 0)
    corr, received, exact, norm_b, raw_near = together(
        (corr, received, exact, norm_b, raw_near)
    )
    diag = diagonal(0)
    for blocks, line in zip(zip(*received), exact):
        block = jnp.concatenate(blocks, 0).astype(f32)
        corr = corr + jnp.where(diag, line.reshape(narrow, 1), block)
    corr = corr / count
    loss = jnp.sum(jnp.where(diag, (1.0 - corr) ** 2, lam * corr * corr))
    gcorr = jnp.where(diag, 2.0 * (corr - 1.0), 2.0 * lam * corr).astype(bf16)

    def line(sums):
        spread = sums[2:3] - sums[3:4] * sums[3:4] / count
        usable = spread > 1e-3 * sums[2:3]
        slope = jnp.where(
            usable,
            (sums[1:2] - sums[0:1] * sums[3:4] / count) / jnp.where(usable, spread, 1.0),
            1.0,
        )
        return slope, (sums[0:1] - slope * sums[3:4]) / count

    stats_a = jnp.stack(
        [
            jnp.sum(gcorr.astype(f32) * sums_b[3].reshape(narrow, 1), axis=0),
            jnp.sum(gcorr.astype(f32) * corr, axis=0),
            jnp.full((half,), loss),
        ]
    )

    moving = [gcorr[:, lo:hi] for lo, hi in cuts(half)]
    cuts_g = (0, 3 * narrow // 8, 3 * narrow // 4, narrow)
    mean_ah, inv_ah = mean_ap[:, :half], inv_ap[:, :half]
    turned, sibling = [], []
    for step in range(3):
        arrived = send(moving, step)
        piece = gcorr[cuts_g[step] : cuts_g[step + 1]]
        if step < 2:
            turned.append(turns(piece))
        else:
            both = [
                turn(jnp.concatenate([piece, x[:, :half]], 0), s + 1)
                for s, x in enumerate(parts_a[1:])
            ]
            turned.append([x[: narrow // 4] for x in both])
            far_0 = [x[narrow // 4 :] for x in both]
        if step == 0:
            for bit in (1, 2):
                stats_a = stats_a + swap_k(stats_a, bit)
            sums_a = sums_a + moments(*raw_near, orders, mean_ap[:, :wide], inv_ap[:, :wide])
            moving, arrived, turned, gcorr, parts_a, stats_a, sums_a, corr = together(
                (moving, arrived, turned, gcorr, parts_a, stats_a, sums_a, corr)
            )
        elif step == 1:
            sums_a = sums_a[:, :half] + swap(sums_a[:, half:], 1)
            both_g = jnp.sum(gcorr.astype(f32) * corr, axis=1)
            near_block = [swap(jnp.concatenate([gcorr] + turned[0], 0), 1)]
            sibling.append(
                [
                    near_block[0][narrow + s * cuts_g[1] : narrow + (s + 1) * cuts_g[1]]
                    for s in range(cubes - 1)
                ]
            )
            own = jnp.concatenate([gcorr, near_block[0][:narrow]], 1)
            moving, arrived, turned, gcorr, sibling, parts_a, own, stats_a, sums_a, both_g = together(
                (moving, arrived, turned, gcorr, sibling, parts_a, own, stats_a, sums_a, both_g)
            )
        else:
            cross = cross_products(0, norm_b, moving, orders, k)
            grad_nb = dot(near, own, ((1,), (1,)))
            stats_b = jnp.stack([jnp.sum(gcorr.astype(f32) * sums_a[3:4], axis=1), both_g])
            stats_a = stats_a + swap_k(stats_a, 4)
            line_a, line_b = line(sums_a), line(sums_b)
            (
                arrived, turned, sibling, far_0, cross, mean_ah, inv_ah, grad_nb, stats_a, stats_b,
                line_a, line_b,
            ) = together(
                (
                    arrived, turned, sibling, far_0, cross, mean_ah, inv_ah, grad_nb, stats_a,
                    stats_b, line_a, line_b,
                )
            )
        if step < 2:
            moving = double(moving, arrived)

    for step in (1, 2):
        sibling.append([swap(x, 1) for x in turned[step]])
    loss = jnp.broadcast_to(stats_a[2:3, :128], (8, 128))
    first_a = stats_a[0:1] / count
    second_a = line_a[0] * stats_a[1:2] + line_a[1] * first_a
    all_a = jnp.concatenate([parts_a[0][:, :half]] + far_0 + [other_a], 0)
    out_a = cross_products(
        1, norm_b, arrived, orders, k, cross, all_a, mean_ah, inv_ah, first_a, second_a
    )
    out_a, stats_b, sibling, rest, loss = together((out_a, stats_b, sibling, rest, loss))
    for mask in h_masks:
        stats_b = stats_b + swap(stats_b, mask)

    for s in range(1, cubes):
        for side, blocks in enumerate((turned, sibling)):
            block = jnp.concatenate([x[cubes - s - 1] for x in blocks], 0)
            start = (s - 1) * wide + side * half
            grad_nb = grad_nb + dot(rest[:, start : start + half], block, ((1,), (1,)))

    mine = cubes * rows
    both = jnp.concatenate([out_a[:mine], swap(out_a[mine:], 1)], 1)
    both, grad_nb, loss, stats_b = together((both, grad_nb, loss, stats_b))
    stats_b = stats_b + swap(stats_b, 1)
    loss = loss + swap(loss, 1)
    first_b = stats_b[0:1] / count
    second_b = line_b[0] * stats_b[1:2] + line_b[1] * first_b
    for mask in h_masks:
        loss = loss + swap(loss, mask)
    blocks = [both[s * rows : (s + 1) * rows] for s in range(cubes)]
    blocks = [blocks[0]] + [turn(blocks[s], -s) for s in range(1, cubes)]
    grad_a = place(blocks, jnp.stack(at))
    out_b = exchange(finish(grad_nb, near_b, mean_bn, inv_bn, first_b, second_b, k))
    grad_b = jnp.concatenate([out_b[r] for r in range(cube)], 1)
    return (loss[0, 0], grad_a, grad_b)


def solution(mesh):
    return jax.shard_map(
        shards,
        mesh=mesh,
        in_specs=(P("dp", None), P("dp", None)),
        out_specs=(P(), P("dp", None), P("dp", None)),
        check_vma=False,
    )
```

```python
import functools
import math

import jax
import jax.numpy as jnp
from jax import lax
from jax.experimental import pallas as pl
from jax.experimental.pallas import tpu as pltpu
from jax.sharding import PartitionSpec as P

lam = 0.0051
eps = 1e-05

cube = 8
orders = ((4, 2, 1), (1, 4, 2), (2, 1, 4))
together = lax.optimization_barrier
strip = 32
vmem = pl.BlockSpec(memory_space=pltpu.VMEM)
smem = pl.BlockSpec(memory_space=pltpu.SMEM)


def room(*arrays):
    sizes = [math.prod(x.shape) * x.dtype.itemsize for x in arrays]
    return pltpu.CompilerParams(vmem_limit_bytes=sum(sizes) + max(sizes) + (4 << 20))


def strips(rows, body, init=None):
    return lax.fori_loop(
        0, rows // strip, lambda i, carry: body(pl.multiple_of(i * strip, strip), carry), init
    )


def places(order):
    return [
        sum(bit for step, bit in enumerate(order) if place >> step & 1) for place in range(cube)
    ]


def cuts(width):
    part = -(-width // 384) * 128
    edges = list(range(0, width, part)) + [width]
    return list(zip(edges, edges[1:]))


def prepare_kernel(half, at_ref, a_ref, b_ref, *outs):
    near_ref, rest_ref, eighths_ref, sums_ref = outs[:4]
    rows, width = a_ref.shape
    for n in range(width // half):
        column = a_ref[:, pl.ds(pl.multiple_of(at_ref[n] * half, half), half)]
        if n < 2:
            near_ref[:, n * half : (n + 1) * half] = column
        else:
            rest_ref[:, (n - 2) * half : (n - 1) * half] = column
    parts = iter(outs[4:])
    for full_ref in (near_ref, rest_ref):
        for lo, hi in cuts(full_ref.shape[1]):
            next(parts)[...] = full_ref[:, lo:hi]
    narrow = width // cube
    for i in range(cube):
        here = slice(i * narrow, (i + 1) * narrow)
        eighths_ref[i] = b_ref[:, here]
        for n, ref in enumerate((a_ref, b_ref)):
            x = ref[:, here].astype(jnp.float32)
            sums_ref[2 * n : 2 * n + 1, here] = jnp.sum(x, axis=0, keepdims=True)
            sums_ref[2 * n + 1 : 2 * n + 2, here] = jnp.sum(x * x, axis=0, keepdims=True)


def prepare(view_a, view_b, at, half):
    rows, width = view_a.shape
    widths = [2 * half, width - 2 * half]
    shapes = [(rows, n) for n in widths] + [(cube, rows, width // cube)]
    parts = [(rows, hi - lo) for n in widths for lo, hi in cuts(n)]
    outs = [jax.ShapeDtypeStruct(shape, jnp.bfloat16) for shape in shapes]
    outs += [jax.ShapeDtypeStruct((4, width), jnp.float32)]
    outs += [jax.ShapeDtypeStruct(shape, jnp.bfloat16) for shape in parts]
    near, rest, eighths, sums, *parts = pl.pallas_call(
        functools.partial(prepare_kernel, half),
        out_shape=outs,
        in_specs=[smem, vmem, vmem],
        out_specs=[vmem] * len(outs),
        compiler_params=room(view_a, view_b, *outs),
    )(at, view_a, view_b)
    first = len(cuts(widths[0]))
    return near, rest, eighths, sums, parts[:first], parts[first:]


def double_kernel(*refs):
    n = len(refs) // 3
    for x, y, out in zip(refs[:n], refs[n : 2 * n], refs[2 * n :]):
        rows = x.shape[0]

        def body(row, _, x=x, y=y, out=out, rows=rows):
            out[pl.ds(row, strip), :] = x[pl.ds(row, strip), :]
            out[pl.ds(rows + row, strip), :] = y[pl.ds(row, strip), :]

        strips(rows, body)


def double(xs, ys):
    return pl.pallas_call(
        double_kernel,
        out_shape=[jax.ShapeDtypeStruct((2 * x.shape[0], x.shape[1]), x.dtype) for x in xs],
        in_specs=[vmem] * (2 * len(xs)),
        out_specs=[vmem] * len(xs),
        compiler_params=room(*xs, *ys, *xs, *ys),
    )(*xs, *ys)


def merge_kernel(orders, mean_ref, inv_ref, *refs):
    pieces, out_ref = refs[:-1], refs[-1]
    rows = pieces[0].shape[0] * 2 // cube
    start = 0
    for n, order in enumerate(orders[: len(pieces) // 2]):
        size = pieces[2 * n].shape[1]
        mean, inv = mean_ref[:, start : start + size], inv_ref[:, start : start + size]
        for m, r in enumerate(places(order)):
            piece, first = pieces[2 * n + 2 * m // cube], m % (cube // 2) * rows


            def body(row, _, piece=piece, first=first, r=r, start=start, size=size, mean=mean, inv=inv):
                raw = piece[pl.ds(first + row, strip), :].astype(jnp.float32)
                out_ref[pl.ds(r * rows + row, strip), start : start + size] = (
                    (raw - mean) * inv
                ).astype(jnp.bfloat16)

            strips(rows, body)
        start += size


def merge(moving, arrived, orders, mean, inv):
    pieces = [x for pair in zip(moving, arrived) for x in pair]
    return pl.pallas_call(
        functools.partial(merge_kernel, orders),
        out_shape=jax.ShapeDtypeStruct((2 * pieces[0].shape[0], mean.shape[1]), jnp.bfloat16),
        in_specs=[vmem] * (2 + len(pieces)),
        out_specs=vmem,
        compiler_params=room(*pieces, *pieces),
    )(mean, inv, *pieces)


def moments_kernel(orders, mean_ref, inv_ref, *refs):
    pieces, out_ref = refs[:-1], refs[-1]
    start = 0
    for n in range(len(pieces) // 2):
        size = pieces[2 * n].shape[1]
        here = slice(start, start + size)
        mean, inv = mean_ref[:, here], inv_ref[:, here]
        total = [jnp.zeros((8, size), jnp.float32)] * 4
        for piece in pieces[2 * n : 2 * n + 2]:

            def body(row, total, piece=piece, mean=mean, inv=inv):
                raw = piece[pl.ds(row, strip), :].astype(jnp.float32)
                flat = (raw - mean) * inv
                norm = flat.astype(jnp.bfloat16).astype(jnp.float32)
                terms = (flat, flat * norm, norm * norm, norm)
                return [
                    t + sum(x[m : m + 8, :] for m in range(0, strip, 8))
                    for t, x in zip(total, terms)
                ]

            total = strips(piece.shape[0], body, total)
        total = [jnp.sum(x, axis=0, keepdims=True) for x in total]
        out_ref[:, here] = jnp.concatenate(total, 0)
        start += size


def moments(moving, arrived, orders, mean, inv):
    pieces = [x for pair in zip(moving, arrived) for x in pair]
    return pl.pallas_call(
        functools.partial(moments_kernel, orders),
        out_shape=jax.ShapeDtypeStruct((4, mean.shape[1]), jnp.float32),
        in_specs=[vmem] * (2 + len(pieces)),
        out_specs=vmem,
        compiler_params=room(*pieces),
    )(mean, inv, *pieces)


def arrange_kernel(k_ref, blocks_ref, mean_ref, inv_ref, raw_ref, norm_ref):
    rows = blocks_ref.shape[1]
    for r in range(cube):

        def body(row, _, r=r):
            raw = blocks_ref[k_ref[0] ^ r, pl.ds(row, strip), :]
            raw_ref[pl.ds(r * rows + row, strip), :] = raw
            norm_ref[pl.ds(r * rows + row, strip), :] = (
                (raw.astype(jnp.float32) - mean_ref[...]) * inv_ref[...]
            ).astype(jnp.bfloat16)

        strips(rows, body)


def arrange(blocks, mean, inv, k):
    _, rows, n = blocks.shape
    out = jax.ShapeDtypeStruct((cube * rows, n), jnp.bfloat16)
    return pl.pallas_call(
        arrange_kernel,
        out_shape=(out, out),
        in_specs=[smem] + [vmem] * 3,
        out_specs=(vmem, vmem),
        compiler_params=room(blocks, out, out),
    )(k.reshape(1), blocks, mean, inv)


def finish_kernel(k_ref, grad_ref, raw_ref, mean_ref, inv_ref, first_ref, second_ref, out_ref):
    rows = out_ref.shape[1]
    mean, inv = mean_ref[...], inv_ref[...]
    for r in range(cube):

        def body(row, _, r=r):
            here = pl.ds(r * rows + row, strip)
            flat = (raw_ref[here, :].astype(jnp.float32) - mean) * inv
            out = inv * (grad_ref[here, :] - first_ref[...] - flat * second_ref[...])
            out_ref[k_ref[0] ^ r, pl.ds(row, strip), :] = out.astype(jnp.bfloat16)

        strips(rows, body)


def finish(grad, raw, mean, inv, first, second, k):
    size, n = grad.shape
    return pl.pallas_call(
        finish_kernel,
        out_shape=jax.ShapeDtypeStruct((cube, size // cube, n), jnp.bfloat16),
        in_specs=[smem] + [vmem] * 6,
        out_specs=vmem,
        compiler_params=room(grad, raw, raw),
    )(k.reshape(1), grad, raw, mean, inv, first, second)


def place_kernel(at_ref, *refs):
    blocks, out_ref = refs[:-1], refs[-1]
    half = blocks[0].shape[1] // 2
    for n, block in enumerate(blocks):
        for side in range(2):
            start = pl.multiple_of(at_ref[2 * n + side] * half, half)
            out_ref[:, pl.ds(start, half)] = block[:, side * half : (side + 1) * half]


def place(blocks, at):
    rows, n = blocks[0].shape
    return pl.pallas_call(
        place_kernel,
        out_shape=jax.ShapeDtypeStruct((rows, n * len(blocks)), jnp.bfloat16),
        in_specs=[smem] + [vmem] * len(blocks),
        out_specs=vmem,
        compiler_params=room(*blocks, *blocks),
    )(at, *blocks)


def dot(x, y, contract):
    return lax.dot_general(x, y, (contract, ((), ())), preferred_element_type=jnp.float32)


def cross_kernel(side, orders, k_ref, rows_ref, *refs):
    if side == 0:
        pieces, out_ref = refs[:-1], refs[-1]
    else:
        total_ref, raw_ref, mean_ref, inv_ref, first_ref, second_ref, *pieces, out_ref = refs
    narrow = rows_ref.shape[1] // cube
    start = 0
    for order, piece in zip(orders, pieces):
        here = slice(start, start + piece.shape[1])
        start += piece.shape[1]
        total = 0.0 if side == 0 else total_ref[:, here]
        for m in range(cube // 2):
            r = places(order)[side * cube // 2 + m]
            at = pl.multiple_of((k_ref[0] ^ r) * narrow, narrow)
            total = total + jnp.dot(
                rows_ref[:, pl.ds(at, narrow)],
                piece[m * narrow : (m + 1) * narrow, :],
                preferred_element_type=jnp.float32,
            )
        if side == 0:
            out_ref[:, here] = total
        else:
            inv = inv_ref[:, here]
            flat = (raw_ref[:, here].astype(jnp.float32) - mean_ref[:, here]) * inv
            out = inv * (total - first_ref[:, here] - flat * second_ref[:, here])
            out_ref[:, here] = out.astype(jnp.bfloat16)


def cross_products(side, rows, pieces, orders, k, *more):
    size, n = rows.shape[0], sum(x.shape[1] for x in pieces)
    block = min(size, 512)

    def whole(x):
        return pl.BlockSpec(x.shape, lambda i: (0, 0))

    def part(x):
        return pl.BlockSpec((block, x.shape[1]), lambda i: (i, 0))

    out = jax.ShapeDtypeStruct((size, n), jnp.bfloat16 if side else jnp.float32)
    specs = [part(x) if x.shape[0] == size else whole(x) for x in more]
    return pl.pallas_call(
        functools.partial(cross_kernel, side, orders),
        grid=(size // block,),
        out_shape=out,
        in_specs=[smem, part(rows)] + specs + [whole(x) for x in pieces],
        out_specs=part(out),
        cost_estimate=pl.CostEstimate(
            flops=size * n * rows.shape[1], bytes_accessed=16 * size * n, transcendentals=0
        ),
        compiler_params=pltpu.CompilerParams(vmem_limit_bytes=48 << 20),
    )(k.reshape(1), rows, *more, *pieces)


def shards(view_a, view_b):
    f32, bf16 = jnp.float32, jnp.bfloat16
    rows, width = view_a.shape
    devices = lax.axis_size("dp")
    count = rows * devices
    cubes = devices // (2 * cube)
    index = lax.axis_index("dp")
    c, k, h = index % 2, index // 2 % cube, index // (2 * cube)
    wide, half, narrow = width // cubes, width // cubes // 2, width // cube
    groups = [
        [(g * cube + i) * 2 + core for i in range(cube)] for g in range(cubes) for core in range(2)
    ]

    def swap(x, mask):
        return lax.ppermute(x, "dp", [(i, i ^ mask) for i in range(devices)])

    def swap_k(x, bit):
        return swap(x, 2 * bit)

    def turn(x, step):
        return lax.ppermute(
            x, "dp", [(i, (i + 2 * cube * step) % devices) for i in range(devices)]
        )

    def turns(x):
        return [turn(x, s) for s in range(1, cubes)]

    def exchange(x):
        return lax.all_to_all(
            x, "dp", split_axis=0, concat_axis=0, axis_index_groups=groups, tiled=True
        )

    def columns(x, start, size):
        return lax.dynamic_slice_in_dim(x, start, size, axis=1)

    at = [(h + s) % cubes * 2 + core for s in range(cubes) for core in (c, 1 - c)]

    h_masks = [2 * cube << bit for bit in range(cubes.bit_length() - 1)]

    def by_place(x, sides):
        return jnp.concatenate([columns(x, place * half, half) for place in sides], 1)

    def send(moving, step):
        return [swap_k(x, order[step]) for x, order in zip(moving, orders)]

    whole_near, whole_rest, eighths, sums, near, rest = prepare(view_a, view_b, jnp.stack(at), half)
    parts_a = [whole_near] + [whole_rest[:, s * wide : (s + 1) * wide] for s in range(cubes - 1)]
    cuts_b = (0, rows // 2, rows)
    pieces_b = [view_b[lo:hi] for lo, hi in zip(cuts_b, cuts_b[1:])]
    others_b = []

    arrived = send(rest, 0)

    own_b = exchange(eighths)
    far_1 = [turn(x[:, half:], s + 1) for s, x in enumerate(parts_a[1:])]
    for mask in h_masks + [1]:
        sums = sums + swap(sums, mask)
    rest, arrived, sums, pieces_b, near, parts_a, far_1 = together(
        (rest, arrived, sums, pieces_b, near, parts_a, far_1)
    )
    rest = double(rest, arrived)
    arrived = send(rest, 1)
    others_b.append(turns(pieces_b[0]))
    for mask in (2, 4):
        sums = sums + swap(sums, mask)
    rest, arrived, others_b, sums, pieces_b, own_b, parts_a, far_1 = together(
        (rest, arrived, others_b, sums, pieces_b, own_b, parts_a, far_1)
    )
    rest = double(rest, arrived)
    arrived = send(rest, 2)
    others_b.append(turns(pieces_b[1]))
    sums = sums + swap(sums, 8)
    means = sums / count
    mean_a, mean_b = means[0:1], means[2:3]
    inv_a = 1.0 / jnp.sqrt(means[1:2] - mean_a * mean_a + eps)
    inv_b = 1.0 / jnp.sqrt(means[3:4] - mean_b * mean_b + eps)
    mean_bn = columns(mean_b, k * narrow, narrow)
    inv_bn = columns(inv_b, k * narrow, narrow)
    mean_ap, inv_ap = by_place(mean_a, at), by_place(inv_a, at)
    near_b, right = arrange(own_b, mean_bn, inv_bn, k)
    rest, arrived, others_b, near_b, right, mean_ap, inv_ap, parts_a, far_1 = together(
        (rest, arrived, others_b, near_b, right, mean_ap, inv_ap, parts_a, far_1)
    )

    def product(left, s):
        first = dot(right, left[:, s * wide + half : (s + 1) * wide], ((0,), (0,)))
        return swap(first, 1) + dot(right, left[:, s * wide : s * wide + half], ((0,), (0,)))

    def diagonal(s):
        return (
            lax.broadcasted_iota(jnp.int32, (narrow, half), 1) + at[2 * s] * half
            == lax.broadcasted_iota(jnp.int32, (narrow, half), 0) + k * narrow
        )

    raw_rest = (rest, arrived)
    rest = merge(rest, arrived, orders, mean_ap[:, wide:], inv_ap[:, wide:])
    arrived = send(near, 0)
    partials = [product(rest, s) for s in range(cubes - 1)]
    exact = [
        jnp.sum(jnp.where(diagonal(s + 1), x, 0.0), axis=1).reshape(1, narrow)
        for s, x in enumerate(partials)
    ]
    partials = [x.astype(bf16) for x in partials]
    partials, exact, near, arrived, others_b, raw_rest, near_b = together(
        (partials, exact, near, arrived, others_b, raw_rest, near_b)
    )
    near = double(near, arrived)

    cuts_p = (0, 3 * narrow // 8, 7 * narrow // 8, narrow)
    received = []
    for step in (1, 2):
        arrived = send(near, step)
        received.append(
            [turn(x[cuts_p[step - 1] : cuts_p[step]], s + 1) for s, x in enumerate(partials)]
        )
        if step == 1:
            other_a = swap(jnp.concatenate([parts_a[0][:, half:]] + far_1, 0), 1)
            flat_b = (near_b.astype(f32) - mean_bn) * inv_bn
            wide_b = flat_b.astype(bf16).astype(f32)
            sums_b = jnp.stack(
                [jnp.sum(x, axis=0) for x in (flat_b, flat_b * wide_b, wide_b * wide_b, wide_b)]
            )
            sums_b = sums_b + swap(sums_b, 1)
            sums_a = moments(*raw_rest, orders, mean_ap[:, wide:], inv_ap[:, wide:])
            near, arrived, received, partials, exact, others_b, other_a, sums_a, sums_b = together(
                (near, arrived, received, partials, exact, others_b, other_a, sums_a, sums_b)
            )
            near = double(near, arrived)
        else:
            others_b = [jnp.concatenate(pieces, 0) for pieces in zip(*others_b)]
            pair_b = jnp.concatenate([view_b] + others_b, 0)
            pair_b = ((pair_b.astype(f32) - mean_b) * inv_b).astype(bf16)
            far_sums = [
                turn(jnp.concatenate([sums_a[:, s * wide : (s + 1) * wide], sums_b], 1), s + 1)
                for s in range(cubes - 1)
            ]
            near, arrived, received, partials, exact, pair_b, far_sums = together(
                (near, arrived, received, partials, exact, pair_b, far_sums)
            )
            sums_a = sum(x[:, :wide] for x in far_sums)
            sums_b = sums_b + sum(x[:, wide:] for x in far_sums)
    received.append([turn(x[cuts_p[2] :], s + 1) for s, x in enumerate(partials)])
    exact = [turn(x, s + 1) for s, x in enumerate(exact)]
    raw_near = (near, arrived)
    near = merge(near, arrived, orders, mean_ap[:, :wide], inv_ap[:, :wide])
    norm_b = jnp.concatenate([pair_b, swap(pair_b, 1)], 0)
    corr = product(near, 0)
    corr, received, exact, norm_b, raw_near = together(
        (corr, received, exact, norm_b, raw_near)
    )
    diag = diagonal(0)
    for blocks, line in zip(zip(*received), exact):
        block = jnp.concatenate(blocks, 0).astype(f32)
        corr = corr + jnp.where(diag, line.reshape(narrow, 1), block)
    corr = corr / count
    loss = jnp.sum(jnp.where(diag, (1.0 - corr) ** 2, lam * corr * corr))
    gcorr = jnp.where(diag, 2.0 * (corr - 1.0), 2.0 * lam * corr).astype(bf16)

    def line(sums):
        spread = sums[2:3] - sums[3:4] * sums[3:4] / count
        usable = spread > 1e-3 * sums[2:3]
        slope = jnp.where(
            usable,
            (sums[1:2] - sums[0:1] * sums[3:4] / count) / jnp.where(usable, spread, 1.0),
            1.0,
        )
        return slope, (sums[0:1] - slope * sums[3:4]) / count

    stats_a = jnp.stack(
        [
            jnp.sum(gcorr.astype(f32) * sums_b[3].reshape(narrow, 1), axis=0),
            jnp.sum(gcorr.astype(f32) * corr, axis=0),
            jnp.full((half,), loss),
        ]
    )

    moving = [gcorr[:, lo:hi] for lo, hi in cuts(half)]
    cuts_g = (0, 3 * narrow // 8, 3 * narrow // 4, narrow)
    mean_ah, inv_ah = mean_ap[:, :half], inv_ap[:, :half]
    turned, sibling = [], []
    for step in range(3):
        arrived = send(moving, step)
        piece = gcorr[cuts_g[step] : cuts_g[step + 1]]
        if step < 2:
            turned.append(turns(piece))
        else:
            both = [
                turn(jnp.concatenate([piece, x[:, :half]], 0), s + 1)
                for s, x in enumerate(parts_a[1:])
            ]
            turned.append([x[: narrow // 4] for x in both])
            far_0 = [x[narrow // 4 :] for x in both]
        if step == 0:
            for bit in (1, 2):
                stats_a = stats_a + swap_k(stats_a, bit)
            sums_a = sums_a + moments(*raw_near, orders, mean_ap[:, :wide], inv_ap[:, :wide])
            moving, arrived, turned, gcorr, parts_a, stats_a, sums_a, corr = together(
                (moving, arrived, turned, gcorr, parts_a, stats_a, sums_a, corr)
            )
        elif step == 1:
            sums_a = sums_a[:, :half] + swap(sums_a[:, half:], 1)
            both_g = jnp.sum(gcorr.astype(f32) * corr, axis=1)
            near_block = [swap(jnp.concatenate([gcorr] + turned[0], 0), 1)]
            sibling.append(
                [
                    near_block[0][narrow + s * cuts_g[1] : narrow + (s + 1) * cuts_g[1]]
                    for s in range(cubes - 1)
                ]
            )
            own = jnp.concatenate([gcorr, near_block[0][:narrow]], 1)
            moving, arrived, turned, gcorr, sibling, parts_a, own, stats_a, sums_a, both_g = together(
                (moving, arrived, turned, gcorr, sibling, parts_a, own, stats_a, sums_a, both_g)
            )
        else:
            cross = cross_products(0, norm_b, moving, orders, k)
            grad_nb = dot(near, own, ((1,), (1,)))
            stats_b = jnp.stack([jnp.sum(gcorr.astype(f32) * sums_a[3:4], axis=1), both_g])
            stats_a = stats_a + swap_k(stats_a, 4)
            line_a, line_b = line(sums_a), line(sums_b)
            (
                arrived, turned, sibling, far_0, cross, mean_ah, inv_ah, grad_nb, stats_a, stats_b,
                line_a, line_b,
            ) = together(
                (
                    arrived, turned, sibling, far_0, cross, mean_ah, inv_ah, grad_nb, stats_a,
                    stats_b, line_a, line_b,
                )
            )
        if step < 2:
            moving = double(moving, arrived)

    for step in (1, 2):
        sibling.append([swap(x, 1) for x in turned[step]])
    loss = jnp.broadcast_to(stats_a[2:3, :128], (8, 128))
    for mask in h_masks:
        stats_b = stats_b + swap(stats_b, mask)
    first_a = stats_a[0:1] / count
    second_a = line_a[0] * stats_a[1:2] + line_a[1] * first_a
    all_a = jnp.concatenate([parts_a[0][:, :half]] + far_0 + [other_a], 0)
    out_a = cross_products(
        1, norm_b, arrived, orders, k, cross, all_a, mean_ah, inv_ah, first_a, second_a
    )
    out_a, stats_b, sibling, rest, loss = together((out_a, stats_b, sibling, rest, loss))
    stats_b = stats_b + swap(stats_b, 1)
    loss = loss + swap(loss, 1)

    for s in range(1, cubes):
        for side, blocks in enumerate((turned, sibling)):
            block = jnp.concatenate([x[cubes - s - 1] for x in blocks], 0)
            start = (s - 1) * wide + side * half
            grad_nb = grad_nb + dot(rest[:, start : start + half], block, ((1,), (1,)))

    mine = cubes * rows
    both = jnp.concatenate([out_a[:mine], swap(out_a[mine:], 1)], 1)
    both, grad_nb, loss, stats_b = together((both, grad_nb, loss, stats_b))
    first_b = stats_b[0:1] / count
    second_b = line_b[0] * stats_b[1:2] + line_b[1] * first_b
    for mask in h_masks:
        loss = loss + swap(loss, mask)
    blocks = [both[s * rows : (s + 1) * rows] for s in range(cubes)]
    blocks = [blocks[0]] + [turn(blocks[s], -s) for s in range(1, cubes)]
    grad_a = place(blocks, jnp.stack(at))
    out_b = exchange(finish(grad_nb, near_b, mean_bn, inv_bn, first_b, second_b, k))
    grad_b = jnp.concatenate([out_b[r] for r in range(cube)], 1)
    return (loss[0, 0], grad_a, grad_b)


def solution(mesh):
    return jax.shard_map(
        shards,
        mesh=mesh,
        in_specs=(P("dp", None), P("dp", None)),
        out_specs=(P(), P("dp", None), P("dp", None)),
        check_vma=False,
    )
```
